128 devices in a mesh: slab: 16 (over x_hi, y, core), cross: 8 (over x_lo, z).
Axes of the slice: x: 4 (x_hi: 2, x_lo: 2; x = x_hi * 2 + x_lo), y: 4, z: 4, core: 2. Of those that a mesh axis runs over, the one named last changes fastest.
Arguments:
- velocity: float32 [3, 256, 256, 256], P(None, 'slab', 'cross'), may hold values from -6 to 6
- pressure: float32 [256, 256, 256], P('slab', 'cross'), may hold values from -6 to 6
- inv_influence: bfloat16 [16384, 16384], P('cross', 'slab'), may hold values from -0.046875 to 0.046875
- normals: float32 [3, 16384], P(None, 'slab'), may hold values from -3 to 3
- sample_cells: int32 [16384, 256], P('slab'), may hold values from 0 to 65535
- tangents: float32 [3, 8, 16, 128], P(None, 'cross', 'slab'), may hold values from -5 to 5
- force_owner: int32 [16384], replicated, may hold values from 0 to 15
- force_cell: int32 [16384], replicated, may hold values from 0 to 8191
Outputs:
- velocity_new: float32 [3, 256, 256, 256], P(None, 'slab', 'cross')
- pressure_new: float32 [256, 256, 256], P('slab', 'cross')
The draws below stay inside these ranges and needn't reach their ends.
Inputs may be any that keep to these rules, and one draw needn't show every extreme that they name: `force_owner`: A few owners take most panels.
All inputs are finite; a program needn't handle non-finite values.
Results may differ from the reference program's by a relative error of at most 0.0003.
Values sent between devices are 32-bit elements; how exact they have to be, the bound alone decides.
A program may use at most 384 MiB of HBM per device.

```python
import math
import jax
import jax.numpy as jnp
import numpy as np
from jax import lax

CX = 16
CY = 32
CZ = 256
NP = 16384
ANGLES = 256
NX = 256
NY = 256
NZ = 256
PANEL_ROWS = 128
N_SLAB = 16
N_CROSS = 8


def place_ends(result, stream_key, least, top_value):
    longest = result.shape.index(max(result.shape))
    spots = []
    for shift in (0, 1):
        where = [jax.random.randint(jax.random.fold_in(stream_key, axis), (), 0, length) for axis, length in enumerate(result.shape)]
        where[longest] = (where[longest] + shift) % result.shape[longest]
        spots.append(tuple(where))
    return result.at[spots[0]].set(least).at[spots[1]].set(top_value)


def block_scale(own_key, shape, cuts, least, top_value):
    loudness = 1.0
    for position, shards_of in cuts:
        steps = jax.random.uniform(jax.random.fold_in(jax.random.fold_in(own_key, 6), position), (shards_of,), jnp.float32, least / len(cuts), top_value / len(cuts))
        loudness = loudness * jnp.repeat(jnp.exp(steps), shape[position] // shards_of).reshape((-1,) + (1,) * (len(shape) - 1 - position))
    return loudness


def cumulative_ranks(number_of, slope):
    loads = [(1 << 20) // math.isqrt(rank ** slope) + 1 for rank in range(1, number_of + 1)]
    scale = 1 + sum(loads) // (1 << 30)
    return np.cumsum(np.array([max(1, weight // scale) for weight in loads]))


def skewed_ids(own_key, shape, count, skew):
    grid = cumulative_ranks(count, skew)
    lot = jax.random.randint(jax.random.fold_in(own_key, 1), shape, 0, int(grid[count - 1]))
    grade = jnp.searchsorted(jnp.asarray(grid, jnp.int32), lot, side="right")
    return jax.random.permutation(jax.random.fold_in(own_key, 2), count)[grade].astype(jnp.int32)


def bell_draw(stream_key, dims, width, bound, split=(), held_as=jnp.bfloat16):
    gain = block_scale(stream_key, dims, split, -0.22, 0.18) if split else 1.0
    result = jax.random.normal(stream_key, dims, jnp.float32) * width * gain
    return jnp.minimum(jnp.maximum(result, -bound), bound).astype(held_as)


def setup_inputs(seed: int = 0) -> dict:
    key_list = jax.random.split(jax.random.key(seed), 9)
    velocity = bell_draw(key_list[0], (3, NX, NY, NZ), 1.0, 6.0, ((1, 16), (2, 8)), jnp.float32)
    pressure = bell_draw(key_list[1], (NX, NY, NZ), 1.0, 6.0, ((0, 16), (1, 8)), jnp.float32)
    inv_influence = bell_draw(key_list[2], (NP, NP), NP ** -0.5, 0.046875, ((0, 8), (1, 16)))
    normals = bell_draw(key_list[3], (3, NP), 0.6, 3.0, ((1, 16),), jnp.float32)
    sample_cells = place_ends(jax.random.randint(key_list[4], (NP, ANGLES), 0, NY * NZ), jax.random.fold_in(key_list[4], 1), 0, (NY * NZ) - 1).astype(jnp.int32)
    tangents = bell_draw(key_list[5], (3, N_CROSS, N_SLAB, PANEL_ROWS), 1.0, 5.0, ((1, 8), (2, 16)), jnp.float32)
    force_owner = place_ends(skewed_ids(key_list[6], (NP,), 2 * N_CROSS, 2), jax.random.fold_in(key_list[6], 3), 0, (2 * N_CROSS) - 1).astype(jnp.int32)
    force_cell = place_ends(jax.random.randint(key_list[7], (NP,), 0, CY * CZ), jax.random.fold_in(key_list[7], 1), 0, (CY * CZ) - 1).astype(jnp.int32)
    return {"velocity": velocity, "pressure": pressure, "inv_influence": inv_influence, "normals": normals, "sample_cells": sample_cells, "tangents": tangents, "force_owner": force_owner, "force_cell": force_cell}


time_step = 0.5
viscosity = 0.1


def padded_all(field):
    return jnp.pad(field, ((0, 0), (1, 1), (1, 1), (1, 1)))


def around_sum(padded):
    total = padded[:, 2:, 1:-1, 1:-1] + padded[:, :-2, 1:-1, 1:-1]
    total = total + padded[:, 1:-1, 2:, 1:-1] + padded[:, 1:-1, :-2, 1:-1]
    return total + padded[:, 1:-1, 1:-1, 2:] + padded[:, 1:-1, 1:-1, :-2]


def slopes(padded, first, second, third):
    slope_x = padded[first, 2:, 1:-1, 1:-1] - padded[first, :-2, 1:-1, 1:-1]
    slope_y = padded[second, 1:-1, 2:, 1:-1] - padded[second, 1:-1, :-2, 1:-1]
    slope_z = padded[third, 1:-1, 1:-1, 2:] - padded[third, 1:-1, 1:-1, :-2]
    return slope_x, slope_y, slope_z


def reference(velocity, pressure, inv_influence, normals, sample_cells, tangents, force_owner, force_cell):
    root_slab = N_SLAB // 2 - 1
    inflow = velocity[:, CX * root_slab + CX // 2].reshape(3, NY * NZ)
    sampled = inflow[:, sample_cells]
    normal_flow = (normals[0][:, None] * sampled[0] + normals[1][:, None] * sampled[1]
                   + normals[2][:, None] * sampled[2]).astype(jnp.bfloat16)
    blocks = inv_influence.reshape(16, NP // 16, NP)
    strength = lax.map(lambda block_rows: jnp.dot(block_rows, normal_flow, preferred_element_type=jnp.float32), blocks)
    strength = strength.reshape(NP, ANGLES)
    loading = jnp.mean(strength * strength, axis=1)
    forces = tangents.reshape(3, NP) * loading[None, :]
    plane_side = force_owner // N_CROSS
    y_index = (force_owner % N_CROSS) * CY + force_cell // CZ
    z_index = force_cell % CZ
    disc = jnp.zeros((3, 2, NY, NZ), jnp.float32).at[:, plane_side, y_index, z_index].add(forces)
    body_force = jnp.zeros_like(velocity)
    body_force = body_force.at[:, CX * root_slab + CX - 1].set(disc[:, 0])
    body_force = body_force.at[:, CX * (root_slab + 1)].set(disc[:, 1])
    predicted = velocity + time_step * (viscosity * (around_sum(padded_all(velocity)) - 6.0 * velocity) + body_force)
    slope_x, slope_y, slope_z = slopes(padded_all(predicted), 0, 1, 2)
    divergence = 0.5 * (slope_x + slope_y + slope_z)
    correction = pressure
    for repeat in range(2):
        correction = (around_sum(padded_all(correction[None]))[0] - divergence) / 6.0
    grad_x, grad_y, grad_z = slopes(padded_all(correction[None]), 0, 0, 0)
    velocity_new = predicted - 0.5 * jnp.stack([grad_x, grad_y, grad_z])
    return velocity_new, correction
```

```python
import functools

import jax
import jax.numpy as jnp
from jax import lax
from jax.experimental import pallas as pl
from jax.experimental.pallas import tpu as pltpu
from jax.sharding import PartitionSpec as P

MESH = pl.DeviceIdType.MESH
F32 = jnp.float32
BF16 = jnp.bfloat16
SIXTH = 1.0 / 6.0
CHUNKS = 4
GROUP = 4


def z_next(a):
    lane = lax.broadcasted_iota(jnp.int32, a.shape, 1)
    return jnp.where(lane == 255, 0.0, pltpu.roll(a, 255, 1))


def z_prev(a):
    lane = lax.broadcasted_iota(jnp.int32, a.shape, 1)
    return jnp.where(lane == 0, 0.0, pltpu.roll(a, 1, 1))


def y_next(a, edge):
    n = a.shape[0]
    row = lax.broadcasted_iota(jnp.int32, a.shape, 0)
    return jnp.where(row == n - 1, edge, pltpu.roll(a, n - 1, 0))


def y_prev(a, edge):
    n = a.shape[0]
    row = lax.broadcasted_iota(jnp.int32, a.shape, 0)
    return jnp.where(row == 0, edge, pltpu.roll(a, 1, 0))


def kernel(
    vel, pres, inv, nrm, cells, tang, owner, cell,
    vel_out, pres_out,
    V, P0, PR, P1, P2, DV, OV,
    EDGE_S, EDGE_R,
    PL, T, A, CI, ZB, YH, YL, NS, TG, KO, KC, RK, ZK,
    NFS, NF, NFB, SB, RB1, SB2, RB2, FB, FA, LHS, RHS, ACC,
    load_sem, ns_sem, a1s, a1r, a2s, a2r, a3s, a3r, ns, nr, e1s, e1r, e2s, e2r,
    f1s, f1r, f2s, f2r, xs, xr, ys, yr, out_sem,
):
    slab = lax.axis_index("slab")
    cross = lax.axis_index("cross")
    h = lax.rem(slab, 2)
    chip = slab // 2
    sib = slab + 1 - 2 * h

    def remote(src, dst, ss, rs, s, c):
        return pltpu.make_async_remote_copy(
            src_ref=src, dst_ref=dst, send_sem=ss, recv_sem=rs, device_id=(s, c), device_id_type=MESH
        )

    def cr(d):
        return lax.rem(cross + d, 8)

    def sl(d):
        return lax.rem(slab + d, 16)

    loads = [
        pltpu.make_async_copy(vel, V.at[:, pl.ds(1, 16)], load_sem.at[0]),
        pltpu.make_async_copy(pres, P0.at[pl.ds(1, 16)], load_sem.at[1]),
        pltpu.make_async_copy(cells.at[pl.ds(pl.multiple_of(cross * 128, 128), 128)], CI, load_sem.at[2]),
        pltpu.make_async_copy(nrm.at[cross], NS, load_sem.at[3]),
        pltpu.make_async_copy(inv, A, load_sem.at[4]),
        pltpu.make_async_copy(tang, TG, load_sem.at[5]),
        pltpu.make_async_copy(owner, KO, load_sem.at[6]),
        pltpu.make_async_copy(cell, KC, load_sem.at[7]),
    ]
    for load in loads:
        load.start()

    barrier = pltpu.get_barrier_semaphore()
    for d in range(1, 16):
        pl.semaphore_signal(barrier, inc=1, device_id=(sl(d), cross), device_id_type=MESH)
    for d in range(1, 8):
        pl.semaphore_signal(barrier, inc=1, device_id=(slab, cr(d)), device_id_type=MESH)
    pl.semaphore_wait(barrier, 22)

    def a1_copy(target):
        half = target % 2
        return remote(
            vel.at[:, 8, pl.ds(half * 16, 16)],
            PL.at[:, pl.ds(pl.multiple_of(cross * 32 + half * 16, 16), 16)],
            a1s.at[target], a1r.at[0], target, cross,
        )

    def tile(c, half):
        return PL.at[:, pl.ds(pl.multiple_of(c * 32 + half * 16, 16), 16)]

    others = [t for t in (6, 8, 5, 4, 9, 2, 1, 3, 0, 10, 14, 15, 11, 13, 12)]

    @pl.when(slab == 7)
    def _():
        for t in others:
            a1_copy(t).start()
        own = pltpu.make_async_copy(vel.at[:, 8, pl.ds(16, 16)], tile(cross, 1), a1r.at[0])
        own.start()

    def x_pair(src_hi, dst_lo, src_lo, dst_hi, k):
        up = remote(src_hi, dst_lo, xs.at[k, 0], xr.at[k, 0], sl(1), cross)
        down = remote(src_lo, dst_hi, xs.at[k, 1], xr.at[k, 1], sl(15), cross)
        return up, down

    def y_pair(k):
        up = remote(EDGE_S.at[k, 0], EDGE_R.at[k, 0], ys.at[k, 0], yr.at[k, 0], slab, cr(1))
        down = remote(EDGE_S.at[k, 1], EDGE_R.at[k, 1], ys.at[k, 1], yr.at[k, 1], slab, cr(7))
        return up, down

    pairs = [x_pair(vel.at[:, 15], V.at[:, 0], vel.at[:, 0], V.at[:, 17], 0),
             x_pair(pres.at[15], P0.at[0], pres.at[0], P0.at[17], 1)]
    for pair in pairs:
        for copy in pair:
            copy.start()

    loads[0].wait()
    loads[1].wait()

    def fill_edges(k, source):
        def step(x, _):
            EDGE_S[k, 0, pl.ds(x, 1), :] = source(x, 31)
            EDGE_S[k, 1, pl.ds(x, 1), :] = source(x, 0)
            return 0
        lax.fori_loop(0, 16, step, 0)

    for i in range(3):
        fill_edges(i, lambda x, r, i=i: V[i, x + 1, r:r + 1, :])
    fill_edges(3, lambda x, r: P0[x + 1, r:r + 1, :])
    v_edges = [y_pair(k) for k in range(4)]
    for pair in v_edges:
        for copy in pair:
            copy.start()

    def finish(pair):
        for copy in pair:
            copy.wait_recv()

    def clear_planes(refs):
        @pl.when(slab == 0)
        def _():
            for ref, lo, hi in refs:
                lo[...] = jnp.zeros(lo.shape, F32)

        @pl.when(slab == 15)
        def _():
            for ref, lo, hi in refs:
                hi[...] = jnp.zeros(hi.shape, F32)

    def clear_rows(ks):
        @pl.when(cross == 0)
        def _():
            for k in ks:
                EDGE_R[k, 0] = jnp.zeros((16, 256), F32)

        @pl.when(cross == 7)
        def _():
            for k in ks:
                EDGE_R[k, 1] = jnp.zeros((16, 256), F32)

    loads[2].wait()
    ci = CI[...]
    ZB[...] = (ci & 255).astype(F32)
    YH[...] = (ci >> 15).astype(F32)
    YL[...] = (ci >> 8) & 127

    a1_in = remote(vel.at[:, 8, pl.ds(0, 16)], tile(cross, h), a1s.at[0], a1r.at[0], slab, cross)
    a1_in.wait_recv()
    a2 = [None] + [
        remote(tile(cross, h), tile(cross, h), a2s.at[d], a2r.at[d], slab, cr(d)) for d in range(1, 8)
    ]
    for d in (4, 1, 7, 3, 5, 2, 6):
        a2[d].start()

    def a3_copy(d):
        src = tile(cr(8 - d), h)
        return remote(src, src, a3s.at[d], a3r.at[d], sib, cross)

    a3_copy(0).start()

    for pair in pairs:
        finish(pair)
    for pair in v_edges:
        finish(pair)
    clear_planes([(V, V.at[:, 0], V.at[:, 17]), (P0, P0.at[0], P0.at[17])])
    clear_rows(range(4))

    def around(u, lo, hi, k, x):
        mid = u(x + 1)
        s = u(x + 2) + u(x)
        s = s + y_next(mid, EDGE_R[k, 1, pl.ds(x, 1), :]) + y_prev(mid, EDGE_R[k, 0, pl.ds(x, 1), :])
        return s + z_next(mid) + z_prev(mid)

    def predict(x, _):
        for i in range(3):
            mid = V[i, x + 1]
            s = around(lambda q: V[i, q], None, None, i, x)
            pr = mid + 0.5 * (0.1 * (s - 6.0 * mid))
            PR[i, x + 1] = pr
            if i == 1:
                EDGE_S[4, 0, pl.ds(x, 1), :] = pr[31:32, :]
                EDGE_S[4, 1, pl.ds(x, 1), :] = pr[0:1, :]
        return 0

    lax.fori_loop(0, 16, predict, 0)
    pr_x = x_pair(PR.at[0, 16], PR.at[0, 0], PR.at[0, 1], PR.at[0, 17], 2)
    pr_y = y_pair(4)
    for copy in pr_x + pr_y:
        copy.start()

    for d in (1, 7, 4, 3, 5, 2, 6):
        remote(tile(cross, h), tile(cr(8 - d), h), a2s.at[d], a2r.at[d], slab, cross).wait_recv()
        a3_copy(d).start()

    finish(pr_x)
    finish(pr_y)
    clear_planes([(PR, PR.at[0, 0], PR.at[0, 17])])
    clear_rows([4])

    def diverge(x, _):
        py = PR[1, x + 1]
        pz = PR[2, x + 1]
        g = PR[0, x + 2] - PR[0, x]
        g = g + (y_next(py, EDGE_R[4, 1, pl.ds(x, 1), :]) - y_prev(py, EDGE_R[4, 0, pl.ds(x, 1), :]))
        g = 0.5 * (g + (z_next(pz) - z_prev(pz)))
        DV[x] = g
        p = (around(lambda q: P0[q], None, None, 3, x) - g) * SIXTH
        P1[x + 1] = p
        EDGE_S[5, 0, pl.ds(x, 1), :] = p[31:32, :]
        EDGE_S[5, 1, pl.ds(x, 1), :] = p[0:1, :]
        return 0

    lax.fori_loop(0, 16, diverge, 0)
    p1_x = x_pair(P1.at[16], P1.at[0], P1.at[1], P1.at[17], 3)
    p1_y = y_pair(5)
    for copy in p1_x + p1_y:
        copy.start()

    for d in (0, 1, 7, 4, 3, 5, 2, 6):
        remote(tile(cross, h), tile(cr(8 - d), 1 - h), a3s.at[d], a3r.at[d], sib, cross).wait_recv()
    for c in range(3):
        for k in range(2):
            T[pl.ds(c * 128, 128), pl.ds(k * 256, 256)] = PL[c, pl.ds(k * 128, 128), :].astype(BF16)

    loads[3].wait()

    row16 = lax.broadcasted_iota(jnp.int32, (16, 16, 256), 0) * 16 + lax.broadcasted_iota(jnp.int32, (16, 16, 256), 1)
    z_of = row16.astype(F32).astype(BF16)
    y_of = lax.broadcasted_iota(jnp.int32, (16, 8, 256), 0) * 8 + lax.broadcasted_iota(jnp.int32, (16, 8, 256), 1)
    rows = 128 // CHUNKS

    def lookup(j):
        zb = jnp.broadcast_to(ZB[pl.ds(j, 1), :], (16, 256)).astype(BF16)[None]
        yh = jnp.broadcast_to(YH[pl.ds(j, 1), :], (16, 256)).astype(BF16)[None]
        mask = z_of == zb
        zero = jnp.zeros((16, 16, 256), BF16)
        one = jnp.ones((1, 16, 256), BF16)
        hot = jnp.concatenate(
            [jnp.where(mask, one - yh, zero).reshape(256, 256), jnp.where(mask, yh, zero).reshape(256, 256)], axis=0
        )
        r = jnp.dot(T[...], hot, preferred_element_type=F32).reshape(3, 16, 8, 256)
        ym = y_of == jnp.broadcast_to(YL[pl.ds(j, 1), :], (8, 256))[None]
        acc = NS[0, j] * jnp.sum(jnp.where(ym, r[0], 0.0), axis=0)
        acc = acc + NS[1, j] * jnp.sum(jnp.where(ym, r[1], 0.0), axis=0)
        acc = acc + NS[2, j] * jnp.sum(jnp.where(ym, r[2], 0.0), axis=0)
        NFS[pl.ds(j, 1), :] = jnp.sum(acc, axis=0, keepdims=True).astype(BF16).astype(F32)

    def nf_copy(d, k):
        part = pl.ds(k * rows, rows)
        return remote(NFS.at[part], NF.at[cross, part], ns.at[d, k], nr.at[d, k], slab, cr(d))

    for k in range(CHUNKS):
        def look(i, _):
            for g in range(GROUP):
                lookup(k * rows + i * GROUP + g)
            return 0
        lax.fori_loop(0, rows // GROUP, look, 0)
        for d in (4, 1, 7, 3, 5, 2, 6):
            nf_copy(d, k).start()

    finish(p1_x)
    finish(p1_y)
    clear_planes([(P1, P1.at[0], P1.at[17])])
    clear_rows([5])

    def sweep(x, _):
        p = (around(lambda q: P1[q], None, None, 5, x) - DV[x]) * SIXTH
        P2[x + 1] = p
        EDGE_S[6, 0, pl.ds(x, 1), :] = p[31:32, :]
        EDGE_S[6, 1, pl.ds(x, 1), :] = p[0:1, :]
        return 0

    lax.fori_loop(0, 16, sweep, 0)
    p2_x = x_pair(P2.at[16], P2.at[0], P2.at[1], P2.at[17], 4)
    p2_y = y_pair(6)
    for copy in p2_x + p2_y:
        copy.start()

    NFB[cross] = NFS[...].astype(BF16)
    for d in range(1, 8):
        src = cr(8 - d)
        for k in range(CHUNKS):
            part = pl.ds(k * rows, rows)
            remote(NFS.at[part], NF.at[src, part], ns.at[d, k], nr.at[d, k], slab, cross).wait_recv()
        NFB[src] = NF[src].astype(BF16)

    loads[4].wait()
    groups = ((1, 2, 3, 4), (5, 6, 7, 0))

    def partial(ds, half):
        lhs = jnp.concatenate([A[lax.rem(chip + d, 8), half] for d in ds], axis=0)
        return jnp.dot(lhs, NFB[...].reshape(1024, 256), preferred_element_type=F32)

    def e1_copy(d):
        return remote(SB.at[d], RB1.at[d], e1s.at[d], e1r.at[d], sib, cross)

    def e2_copy(d):
        return remote(SB2.at[d], RB2.at[d], e2s.at[d], e2r.at[d], lax.rem(chip + d, 8) * 2 + h, cross)

    for ds in groups:
        p = partial(ds, 1 - h)
        for n, d in enumerate(ds):
            SB[d] = p[n * 128:(n + 1) * 128]
            e1_copy(d).start()
    for ds in groups:
        p = partial(ds, h)
        for n, d in enumerate(ds):
            e1_copy(d).wait_recv()
            SB2[d] = p[n * 128:(n + 1) * 128] + RB1[d]
            if d:
                e2_copy(d).start()

    finish(p2_x)
    finish(p2_y)
    clear_planes([(P2, P2.at[0], P2.at[17])])
    clear_rows([6])

    def correct(x, _):
        mid = P2[x + 1]
        OV[0, x] = PR[0, x + 1] - 0.5 * (P2[x + 2] - P2[x])
        gy = y_next(mid, EDGE_R[6, 1, pl.ds(x, 1), :]) - y_prev(mid, EDGE_R[6, 0, pl.ds(x, 1), :])
        OV[1, x] = PR[1, x + 1] - 0.5 * gy
        OV[2, x] = PR[2, x + 1] - 0.5 * (z_next(mid) - z_prev(mid))
        return 0

    lax.fori_loop(0, 16, correct, 0)

    def outs(k, lo, n):
        return [
            pltpu.make_async_copy(OV.at[:, pl.ds(lo, n)], vel_out.at[:, pl.ds(lo, n)], out_sem.at[2 * k]),
            pltpu.make_async_copy(P2.at[pl.ds(lo + 1, n)], pres_out.at[pl.ds(lo, n)], out_sem.at[2 * k + 1]),
        ]

    early = outs(0, 4, 8)
    late = outs(1, 0, 4) + outs(2, 12, 4)
    for copy in early:
        copy.start()

    loads[6].wait()
    loads[7].wait()
    ko = KO[...]
    kc = KC[...]
    rel = (ko & 7) * 32 + (kc >> 8) - (cross * 32 - 4)
    RK[...] = jnp.where((rel >= 0) & (rel < 40), (ko >> 3) * 40 + rel, -1).astype(F32)
    ZK[...] = (kc & 255).astype(F32)

    loads[5].wait()
    total = SB2[0]
    for d in range(1, 8):
        e2_copy(d).wait_recv()
        total = total + RB2[d]
    mean = lax.dot_general(
        jnp.ones((8, 256), F32), total * total, (((1,), (1,)), ((), ())),
        precision=lax.Precision.HIGHEST, preferred_element_type=F32,
    )[0:1] * (1.0 / 256.0)
    FB[...] = TG[...] * mean

    def f1_copy(k):
        return remote(FB, FA.at[cross, slab], f1s.at[k], f1r.at[slab], 7 + k, cross)

    for k in range(2):
        @pl.when(slab != 7 + k)
        def _():
            f1_copy(k).start()

    @pl.when((slab == 7) | (slab == 8))
    def _():
        FA[cross, slab] = FB[...]
        for s in range(16):
            @pl.when(slab != s)
            def _():
                remote(FB, FA.at[cross, s], f1s.at[0], f1r.at[s], slab, cross).wait_recv()

        f2 = [remote(FA.at[cross], FA.at[cross], f2s.at[d], f2r.at[d], slab, cr(d)) for d in range(1, 8)]
        for copy in f2:
            copy.start()

        for d in range(1, 8):
            src = FA.at[cr(8 - d)]
            remote(src, src, f2s.at[d], f2r.at[d], slab, cross).wait_recv()

        r_of = (lax.broadcasted_iota(jnp.int32, (5, 16, 128), 0) * 16
                + lax.broadcasted_iota(jnp.int32, (5, 16, 128), 1)).astype(F32).astype(BF16)
        z_at = (lax.broadcasted_iota(jnp.int32, (16, 16, 128), 0) * 16
                + lax.broadcasted_iota(jnp.int32, (16, 16, 128), 1)).astype(F32).astype(BF16)
        ACC[...] = jnp.zeros(ACC.shape, F32)

        def add(c, _):
            for s in range(16):
                q = c * 16 + s
                lanes = pl.ds(s * 128, 128)
                rk = jnp.broadcast_to(RK[pl.ds(q, 1), :], (16, 128)).astype(BF16)[None]
                zk = jnp.broadcast_to(ZK[pl.ds(q, 1), :], (16, 128)).astype(BF16)[None]
                f = FA[c, s]
                hi = f.astype(BF16).astype(F32)
                lo = f - hi
                mask = r_of == rk
                for i in range(3):
                    for n, part in enumerate((hi, lo)):
                        value = jnp.broadcast_to(part[i:i + 1], (16, 128)).astype(BF16)[None]
                        LHS[pl.ds((i * 2 + n) * 5, 5), :, lanes] = jnp.where(mask, value, jnp.zeros((5, 16, 128), BF16))
                RHS[:, :, lanes] = jnp.where(z_at == zk, jnp.ones((1, 16, 128), BF16), jnp.zeros((16, 16, 128), BF16))
            ACC[...] += lax.dot_general(
                LHS[...].reshape(480, 2048), RHS[...].reshape(256, 2048), (((1,), (1,)), ((), ())),
                preferred_element_type=F32,
            )
            return 0

        lax.fori_loop(0, 8, add, 0)

        push = {}
        for i in range(3):
            for p in range(2):
                at = i * 160 + p * 40
                push[i, 127 + p] = 0.5 * (ACC[at:at + 40, :] + ACC[at + 80:at + 120, :])
        row = lax.broadcasted_iota(jnp.int32, (40, 256), 0) + (cross * 32 - 4)
        inside = (row >= 0) & (row < 256)

        def within(a):
            return jnp.where(inside, a, 0.0)

        def ny(a):
            return pltpu.roll(a, 39, 0)

        def py(a):
            return pltpu.roll(a, 1, 0)

        div = {126: 0.5 * push[0, 127], 129: -0.5 * push[0, 128]}
        for x, side in ((127, push[0, 128]), (128, -push[0, 127])):
            a, b = push[1, x], push[2, x]
            div[x] = within(0.5 * (side + (ny(a) - py(a)) + (z_next(b) - z_prev(b))))
        one = {x: -SIXTH * div[x] for x in div}
        two = {}
        for x in range(125, 131):
            s = None
            if x in one:
                a = one[x]
                s = ny(a) + py(a) + z_next(a) + z_prev(a) - div[x]
            for near in (x - 1, x + 1):
                if near in one:
                    s = one[near] if s is None else s + one[near]
            two[x] = within(s * SIXTH)

        def centre(a):
            return pltpu.roll(a, 36, 0)[0:32]

        def apply(first, local):
            for n in range(4):
                x = first + n
                g = None
                if x + 1 in two:
                    g = two[x + 1]
                if x - 1 in two:
                    g = -two[x - 1] if g is None else g - two[x - 1]
                vx = -0.5 * g
                if x in (127, 128):
                    vx = vx + push[0, x]
                OV[0, local + n] += centre(vx)
                if x in two:
                    a = two[x]
                    P2[local + n + 1] += centre(a)
                    vy = -0.5 * (ny(a) - py(a))
                    vz = -0.5 * (z_next(a) - z_prev(a))
                    if x in (127, 128):
                        vy = vy + push[1, x]
                        vz = vz + push[2, x]
                    OV[1, local + n] += centre(vy)
                    OV[2, local + n] += centre(vz)

        for copy in p2_x:
            copy.wait_send()

        @pl.when(slab == 7)
        def _():
            apply(124, 12)

        @pl.when(slab == 8)
        def _():
            apply(128, 0)

        for copy in f2:
            copy.wait_send()

    for copy in late:
        copy.start()

    @pl.when(slab == 7)
    def _():
        for t in others:
            a1_copy(t).wait_send()
    for d in range(8):
        if d:
            a2[d].wait_send()
            for k in range(CHUNKS):
                nf_copy(d, k).wait_send()
            e2_copy(d).wait_send()
        a3_copy(d).wait_send()
        e1_copy(d).wait_send()
    for pair in pairs + v_edges + [pr_x, pr_y, p1_x, p1_y, p2_y]:
        for copy in pair:
            copy.wait_send()

    @pl.when((slab != 7) & (slab != 8))
    def _():
        for copy in p2_x:
            copy.wait_send()
    for k in range(2):
        @pl.when(slab != 7 + k)
        def _():
            f1_copy(k).wait_send()
    for copy in early + late:
        copy.wait()


def body(velocity, pressure, inv_influence, normals, sample_cells, tangents, force_owner, force_cell):
    any_space = pl.BlockSpec(memory_space=pl.ANY)
    dma = pltpu.SemaphoreType.DMA
    vm = pltpu.VMEM
    return pl.pallas_call(
        kernel,
        out_shape=(
            jax.ShapeDtypeStruct(velocity.shape, F32),
            jax.ShapeDtypeStruct(pressure.shape, F32),
        ),
        in_specs=[any_space] * 8,
        out_specs=(any_space, any_space),
        scratch_shapes=[
            vm((3, 18, 32, 256), F32), vm((18, 32, 256), F32), vm((3, 18, 32, 256), F32),
            vm((18, 32, 256), F32), vm((18, 32, 256), F32), vm((16, 32, 256), F32), vm((3, 16, 32, 256), F32),
            vm((7, 2, 16, 256), F32), vm((7, 2, 16, 256), F32),
            vm((3, 256, 256), F32), vm((384, 512), BF16), vm((8, 2, 128, 1024), BF16), vm((128, 256), jnp.int32),
            vm((128, 256), F32), vm((128, 256), F32), vm((128, 256), jnp.int32),
            pltpu.SMEM((3, 128), F32), vm((3, 128), F32),
            vm((128, 128), jnp.int32), vm((128, 128), jnp.int32), vm((128, 128), F32), vm((128, 128), F32),
            vm((128, 256), F32), vm((8, 128, 256), F32), vm((8, 128, 256), BF16),
            vm((8, 128, 256), F32), vm((8, 128, 256), F32), vm((8, 128, 256), F32), vm((8, 128, 256), F32),
            vm((3, 128), F32), vm((8, 16, 3, 128), F32),
            vm((30, 16, 2048), BF16), vm((16, 16, 2048), BF16), vm((480, 256), F32),
            dma((8,)), dma((1,)), dma((16,)), dma((1,)), dma((8,)), dma((8,)), dma((8,)), dma((8,)),
            dma((8, CHUNKS)), dma((8, CHUNKS)), dma((8,)), dma((8,)), dma((8,)), dma((8,)),
            dma((2,)), dma((16,)), dma((8,)), dma((8,)), dma((5, 2)), dma((5, 2)), dma((7, 2)), dma((7, 2)),
            dma((6,)),
        ],
        compiler_params=pltpu.CompilerParams(
            collective_id=0, has_side_effects=True, vmem_limit_bytes=56 * 1024 * 1024
        ),
    )(
        velocity, pressure, inv_influence.reshape(8, 2, 128, 1024),
        normals.reshape(3, 8, 128).transpose(1, 0, 2), sample_cells, tangents.reshape(3, 128),
        force_owner.reshape(128, 128), force_cell.reshape(128, 128),
    )


def solution(mesh):
    return jax.shard_map(
        body,
        mesh=mesh,
        in_specs=(
            P(None, "slab", "cross", None),
            P("slab", "cross", None),
            P("cross", "slab"),
            P(None, "slab"),
            P("slab", None),
            P(None, "cross", "slab", None),
            P(),
            P(),
        ),
        out_specs=(P(None, "slab", "cross", None), P("slab", "cross", None)),
        check_vma=False,
    )
```

```python
import functools

import jax
import jax.numpy as jnp
from jax import lax
from jax.experimental import pallas as pl
from jax.experimental.pallas import tpu as pltpu
from jax.sharding import PartitionSpec as P

MESH = pl.DeviceIdType.MESH
F32 = jnp.float32
BF16 = jnp.bfloat16
SIXTH = 1.0 / 6.0
CHUNKS = 4
GROUP = 16


def z_next(a):
    lane = lax.broadcasted_iota(jnp.int32, a.shape, 1)
    return jnp.where(lane == 255, 0.0, pltpu.roll(a, 255, 1))


def z_prev(a):
    lane = lax.broadcasted_iota(jnp.int32, a.shape, 1)
    return jnp.where(lane == 0, 0.0, pltpu.roll(a, 1, 1))


def y_next(a, edge):
    n = a.shape[0]
    row = lax.broadcasted_iota(jnp.int32, a.shape, 0)
    return jnp.where(row == n - 1, edge, pltpu.roll(a, n - 1, 0))


def y_prev(a, edge):
    n = a.shape[0]
    row = lax.broadcasted_iota(jnp.int32, a.shape, 0)
    return jnp.where(row == 0, edge, pltpu.roll(a, 1, 0))


def kernel(
    vel, pres, inv, nrm, cells, tang, owner, cell,
    ov_out, p2_out, push_out,
    V, P0, PR, P1, P2, DV, OV,
    EDGE_S, EDGE_R,
    PL, T, A, CI, ZB, YH, YL, NS, TG, KO, KC, RK, ZK,
    NFS, NF, NFB, SB, RB1, SB2, RB2, FB, FA, LHS, RHS, ACC, PUSH,
    load_sem, ns_sem, a1s, a1r, a2s, a2r, a3s, a3r, ns, nr, e1s, e1r, e2s, e2r,
    f1s, f1r, xs, xr, ys, yr, out_sem,
):
    slab = lax.axis_index("slab")
    cross = lax.axis_index("cross")
    h = lax.rem(slab, 2)
    chip = slab // 2
    sib = slab + 1 - 2 * h

    def remote(src, dst, ss, rs, s, c):
        return pltpu.make_async_remote_copy(
            src_ref=src, dst_ref=dst, send_sem=ss, recv_sem=rs, device_id=(s, c), device_id_type=MESH
        )

    def cr(d):
        return lax.rem(cross + d, 8)

    def sl(d):
        return lax.rem(slab + d, 16)

    loads = [
        pltpu.make_async_copy(vel, V.at[:, pl.ds(1, 16)], load_sem.at[0]),
        pltpu.make_async_copy(pres, P0.at[pl.ds(1, 16)], load_sem.at[1]),
        pltpu.make_async_copy(cells.at[pl.ds(pl.multiple_of(cross * 128, 128), 128)], CI, load_sem.at[2]),
        pltpu.make_async_copy(nrm.at[cross], NS, load_sem.at[3]),
        pltpu.make_async_copy(inv, A, load_sem.at[4]),
        pltpu.make_async_copy(tang, TG, load_sem.at[5]),
        pltpu.make_async_copy(owner, KO, load_sem.at[6]),
        pltpu.make_async_copy(cell, KC, load_sem.at[7]),
    ]
    for load in loads:
        load.start()

    barrier = pltpu.get_barrier_semaphore()
    for d in range(1, 16):
        pl.semaphore_signal(barrier, inc=1, device_id=(sl(d), cross), device_id_type=MESH)
    for d in range(1, 8):
        pl.semaphore_signal(barrier, inc=1, device_id=(slab, cr(d)), device_id_type=MESH)
    pl.semaphore_wait(barrier, 22)

    def a1_copy(target):
        half = target % 2
        return remote(
            vel.at[:, 8, pl.ds(half * 16, 16)],
            PL.at[:, pl.ds(pl.multiple_of(cross * 32 + half * 16, 16), 16)],
            a1s.at[target], a1r.at[0], target, cross,
        )

    def tile(c, half):
        return PL.at[:, pl.ds(pl.multiple_of(c * 32 + half * 16, 16), 16)]

    others = [t for t in (6, 8, 5, 4, 9, 2, 1, 3, 0, 10, 14, 15, 11, 13, 12)]

    @pl.when(slab == 7)
    def _():
        for t in others:
            a1_copy(t).start()
        own = pltpu.make_async_copy(vel.at[:, 8, pl.ds(16, 16)], tile(cross, 1), a1r.at[0])
        own.start()
        for t in others:
            a1_copy(t).wait_send()

    def x_pair(src_hi, dst_lo, src_lo, dst_hi, k):
        up = remote(src_hi, dst_lo, xs.at[k, 0], xr.at[k, 0], sl(1), cross)
        down = remote(src_lo, dst_hi, xs.at[k, 1], xr.at[k, 1], sl(15), cross)
        return up, down

    def y_pair(k):
        up = remote(EDGE_S.at[k, 0], EDGE_R.at[k, 0], ys.at[k, 0], yr.at[k, 0], slab, cr(1))
        down = remote(EDGE_S.at[k, 1], EDGE_R.at[k, 1], ys.at[k, 1], yr.at[k, 1], slab, cr(7))
        return up, down

    pairs = [x_pair(vel.at[:, 15], V.at[:, 0], vel.at[:, 0], V.at[:, 17], 0),
             x_pair(pres.at[15], P0.at[0], pres.at[0], P0.at[17], 1)]
    for pair in pairs:
        for copy in pair:
            copy.start()

    loads[0].wait()
    loads[1].wait()

    def fill_edges(k, source):
        def step(x, _):
            EDGE_S[k, 0, pl.ds(x, 1), :] = source(x, 31)
            EDGE_S[k, 1, pl.ds(x, 1), :] = source(x, 0)
            return 0
        lax.fori_loop(0, 16, step, 0)

    for i in range(3):
        fill_edges(i, lambda x, r, i=i: V[i, x + 1, r:r + 1, :])
    fill_edges(3, lambda x, r: P0[x + 1, r:r + 1, :])
    v_edges = [y_pair(k) for k in range(4)]
    for pair in v_edges:
        for copy in pair:
            copy.start()

    def finish(pair):
        for copy in pair:
            copy.wait_recv()

    def clear_planes(refs):
        @pl.when(slab == 0)
        def _():
            for ref, lo, hi in refs:
                lo[...] = jnp.zeros(lo.shape, F32)

        @pl.when(slab == 15)
        def _():
            for ref, lo, hi in refs:
                hi[...] = jnp.zeros(hi.shape, F32)

    def clear_rows(ks):
        @pl.when(cross == 0)
        def _():
            for k in ks:
                EDGE_R[k, 0] = jnp.zeros((16, 256), F32)

        @pl.when(cross == 7)
        def _():
            for k in ks:
                EDGE_R[k, 1] = jnp.zeros((16, 256), F32)

    loads[2].wait()
    ci = CI[...]
    ZB[...] = (ci & 255).astype(F32)
    YH[...] = (ci >> 15).astype(F32)
    YL[...] = (ci >> 8) & 127

    loads[6].wait()
    loads[7].wait()
    ko = KO[...]
    kc = KC[...]
    rel = (ko & 7) * 32 + (kc >> 8) - (cross * 32 - 4)
    RK[...] = jnp.where((rel >= 0) & (rel < 40), (ko >> 3) * 40 + rel, -1).astype(F32)
    ZK[...] = (kc & 255).astype(F32)

    z_at = (lax.broadcasted_iota(jnp.int32, (16, 16, 128), 0) * 16
            + lax.broadcasted_iota(jnp.int32, (16, 16, 128), 1)).astype(F32).astype(BF16)

    @pl.when((slab == 7) | (slab == 8))
    def _():
        def place(c, _):
            for s in range(16):
                zk = jnp.broadcast_to(ZK[pl.ds(c * 16 + s, 1), :], (16, 128)).astype(BF16)[None]
                RHS[c, :, :, s * 128:(s + 1) * 128] = jnp.where(
                    z_at == zk, jnp.ones((1, 16, 128), BF16), jnp.zeros((16, 16, 128), BF16)
                )
            return 0
        lax.fori_loop(0, 8, place, 0)

    a1_in = remote(vel.at[:, 8, pl.ds(0, 16)], tile(cross, h), a1s.at[0], a1r.at[0], slab, cross)
    a1_in.wait_recv()
    a2 = [None] + [
        remote(tile(cross, h), tile(cross, h), a2s.at[d], a2r.at[d], slab, cr(d)) for d in range(1, 8)
    ]
    for d in (4, 1, 7, 3, 5, 2, 6):
        a2[d].start()

    def a3_copy(d):
        src = tile(cr(8 - d), h)
        return remote(src, src, a3s.at[d], a3r.at[d], sib, cross)

    a3_copy(0).start()

    for pair in pairs:
        finish(pair)
    for pair in v_edges:
        finish(pair)
    clear_planes([(V, V.at[:, 0], V.at[:, 17]), (P0, P0.at[0], P0.at[17])])
    clear_rows(range(4))

    def around(u, lo, hi, k, x):
        mid = u(x + 1)
        s = u(x + 2) + u(x)
        s = s + y_next(mid, EDGE_R[k, 1, pl.ds(x, 1), :]) + y_prev(mid, EDGE_R[k, 0, pl.ds(x, 1), :])
        return s + z_next(mid) + z_prev(mid)

    def predict(x, _):
        for i in range(3):
            mid = V[i, x + 1]
            s = around(lambda q: V[i, q], None, None, i, x)
            pr = mid + 0.5 * (0.1 * (s - 6.0 * mid))
            PR[i, x + 1] = pr
            if i == 1:
                EDGE_S[4, 0, pl.ds(x, 1), :] = pr[31:32, :]
                EDGE_S[4, 1, pl.ds(x, 1), :] = pr[0:1, :]
        return 0

    lax.fori_loop(0, 16, predict, 0)
    pr_x = x_pair(PR.at[0, 16], PR.at[0, 0], PR.at[0, 1], PR.at[0, 17], 2)
    pr_y = y_pair(4)
    for copy in pr_x + pr_y:
        copy.start()

    for d in (1, 7, 4, 3, 5, 2, 6):
        remote(tile(cross, h), tile(cr(8 - d), h), a2s.at[d], a2r.at[d], slab, cross).wait_recv()
        a3_copy(d).start()

    for d in (0, 1, 7, 4, 3, 5, 2, 6):
        remote(tile(cross, h), tile(cr(8 - d), 1 - h), a3s.at[d], a3r.at[d], sib, cross).wait_recv()
    for c in range(3):
        for k in range(2):
            T[pl.ds(c * 128, 128), pl.ds(k * 256, 256)] = PL[c, pl.ds(k * 128, 128), :].astype(BF16)

    loads[3].wait()

    row16 = lax.broadcasted_iota(jnp.int32, (16, 16, 256), 0) * 16 + lax.broadcasted_iota(jnp.int32, (16, 16, 256), 1)
    z_of = row16.astype(F32).astype(BF16)
    y_of = lax.broadcasted_iota(jnp.int32, (16, 8, 256), 0) * 8 + lax.broadcasted_iota(jnp.int32, (16, 8, 256), 1)
    rows = 128 // CHUNKS

    def lookup(j):
        zb = jnp.broadcast_to(ZB[pl.ds(j, 1), :], (16, 256)).astype(BF16)[None]
        yh = jnp.broadcast_to(YH[pl.ds(j, 1), :], (16, 256)).astype(BF16)[None]
        mask = z_of == zb
        zero = jnp.zeros((16, 16, 256), BF16)
        one = jnp.ones((1, 16, 256), BF16)
        hot = jnp.concatenate(
            [jnp.where(mask, one - yh, zero).reshape(256, 256), jnp.where(mask, yh, zero).reshape(256, 256)], axis=0
        )
        r = jnp.dot(T[...], hot, preferred_element_type=F32).reshape(3, 16, 8, 256)
        ym = y_of == jnp.broadcast_to(YL[pl.ds(j, 1), :], (8, 256))[None]
        acc = NS[0, j] * jnp.sum(jnp.where(ym, r[0], 0.0), axis=0)
        acc = acc + NS[1, j] * jnp.sum(jnp.where(ym, r[1], 0.0), axis=0)
        acc = acc + NS[2, j] * jnp.sum(jnp.where(ym, r[2], 0.0), axis=0)
        NFS[pl.ds(j, 1), :] = jnp.sum(acc, axis=0, keepdims=True).astype(BF16).astype(F32)

    def nf_copy(d, k):
        part = pl.ds(k * rows, rows)
        return remote(NFS.at[part], NF.at[cross, part], ns.at[d, k], nr.at[d, k], slab, cr(d))

    for k in range(CHUNKS):
        def look(i, _):
            for g in range(GROUP):
                lookup(k * rows + i * GROUP + g)
            return 0
        lax.fori_loop(0, rows // GROUP, look, 0)
        for d in (4, 1, 7, 3, 5, 2, 6):
            nf_copy(d, k).start()

    finish(pr_x)
    finish(pr_y)
    clear_planes([(PR, PR.at[0, 0], PR.at[0, 17])])
    clear_rows([4])

    def diverge(x, _):
        py = PR[1, x + 1]
        pz = PR[2, x + 1]
        g = PR[0, x + 2] - PR[0, x]
        g = g + (y_next(py, EDGE_R[4, 1, pl.ds(x, 1), :]) - y_prev(py, EDGE_R[4, 0, pl.ds(x, 1), :]))
        g = 0.5 * (g + (z_next(pz) - z_prev(pz)))
        DV[x] = g
        p = (around(lambda q: P0[q], None, None, 3, x) - g) * SIXTH
        P1[x + 1] = p
        EDGE_S[5, 0, pl.ds(x, 1), :] = p[31:32, :]
        EDGE_S[5, 1, pl.ds(x, 1), :] = p[0:1, :]
        return 0

    lax.fori_loop(0, 16, diverge, 0)
    p1_x = x_pair(P1.at[16], P1.at[0], P1.at[1], P1.at[17], 3)
    p1_y = y_pair(5)
    for copy in p1_x + p1_y:
        copy.start()

    NFB[cross] = NFS[...].astype(BF16)
    for d in range(1, 8):
        src = cr(8 - d)
        for k in range(CHUNKS):
            part = pl.ds(k * rows, rows)
            remote(NFS.at[part], NF.at[src, part], ns.at[d, k], nr.at[d, k], slab, cross).wait_recv()
        NFB[src] = NF[src].astype(BF16)

    loads[4].wait()
    groups = ((1, 2, 3, 4), (5, 6, 7, 0))

    def partial(ds, half):
        lhs = jnp.concatenate([A[lax.rem(chip + d, 8), half] for d in ds], axis=0)
        return jnp.dot(lhs, NFB[...].reshape(1024, 256), preferred_element_type=F32)

    def e1_copy(d):
        return remote(SB.at[d], RB1.at[d], e1s.at[d], e1r.at[d], sib, cross)

    def e2_copy(d):
        return remote(SB2.at[d], RB2.at[d], e2s.at[d], e2r.at[d], lax.rem(chip + d, 8) * 2 + h, cross)

    for ds in groups:
        p = partial(ds, 1 - h)
        for n, d in enumerate(ds):
            SB[d] = p[n * 128:(n + 1) * 128]
            e1_copy(d).start()
    for ds in groups:
        p = partial(ds, h)
        for n, d in enumerate(ds):
            e1_copy(d).wait_recv()
            SB2[d] = p[n * 128:(n + 1) * 128] + RB1[d]
            if d:
                e2_copy(d).start()

    finish(p1_x)
    finish(p1_y)
    clear_planes([(P1, P1.at[0], P1.at[17])])
    clear_rows([5])

    def sweep(x, _):
        p = (around(lambda q: P1[q], None, None, 5, x) - DV[x]) * SIXTH
        P2[x + 1] = p
        EDGE_S[6, 0, pl.ds(x, 1), :] = p[31:32, :]
        EDGE_S[6, 1, pl.ds(x, 1), :] = p[0:1, :]
        return 0

    lax.fori_loop(0, 16, sweep, 0)
    p2_x = x_pair(P2.at[16], P2.at[0], P2.at[1], P2.at[17], 4)
    p2_y = y_pair(6)
    for copy in p2_x + p2_y:
        copy.start()

    finish(p2_x)
    finish(p2_y)
    clear_planes([(P2, P2.at[0], P2.at[17])])
    clear_rows([6])

    def correct(x, _):
        mid = P2[x + 1]
        OV[0, x] = PR[0, x + 1] - 0.5 * (P2[x + 2] - P2[x])
        gy = y_next(mid, EDGE_R[6, 1, pl.ds(x, 1), :]) - y_prev(mid, EDGE_R[6, 0, pl.ds(x, 1), :])
        OV[1, x] = PR[1, x + 1] - 0.5 * gy
        OV[2, x] = PR[2, x + 1] - 0.5 * (z_next(mid) - z_prev(mid))
        return 0

    lax.fori_loop(0, 16, correct, 0)

    outs = [
        pltpu.make_async_copy(OV, ov_out, out_sem.at[0]),
        pltpu.make_async_copy(P2.at[pl.ds(1, 16)], p2_out, out_sem.at[1]),
    ]
    for copy in outs:
        copy.start()

    loads[5].wait()
    total = SB2[0]
    for d in range(1, 8):
        e2_copy(d).wait_recv()
        total = total + RB2[d]
    mean = lax.dot_general(
        jnp.ones((8, 256), F32), total * total, (((1,), (1,)), ((), ())),
        precision=lax.Precision.HIGHEST, preferred_element_type=F32,
    )[0:1] * (1.0 / 256.0)
    FB[...] = TG[:, 0, 0, :] * mean

    def f1_copy(s, d):
        return remote(FB, FA.at[cross, slab], f1s.at[(s - 7) * 8 + d], f1r.at[0], s, cr(d))

    def f1_sends(act):
        for d in (4, 2, 6, 3, 5, 1, 7, 0):
            for s in (7, 8):
                if d:
                    act(f1_copy(s, d))
                else:
                    @pl.when(slab != s)
                    def _():
                        act(f1_copy(s, 0))

    f1_sends(lambda copy: copy.start())

    @pl.when((slab == 7) | (slab == 8))
    def _():
        pltpu.make_async_copy(FB, FA.at[cross, slab], f1r.at[0]).start()
        remote(FA, FA, f1s.at[0], f1r.at[0], slab, cross).wait_recv()

        r_of = (lax.broadcasted_iota(jnp.int32, (5, 16, 128), 0) * 16
                + lax.broadcasted_iota(jnp.int32, (5, 16, 128), 1)).astype(F32).astype(BF16)
        ACC[...] = jnp.zeros(ACC.shape, F32)

        def add(c, _):
            for s in range(16):
                q = c * 16 + s
                lanes = pl.ds(s * 128, 128)
                rk = jnp.broadcast_to(RK[pl.ds(q, 1), :], (16, 128)).astype(BF16)[None]
                f = FA[c, s]
                hi = f.astype(BF16).astype(F32)
                lo = f - hi
                mask = r_of == rk
                for i in range(3):
                    for n, part in enumerate((hi, lo)):
                        value = jnp.broadcast_to(part[i:i + 1], (16, 128)).astype(BF16)[None]
                        LHS[pl.ds((i * 2 + n) * 5, 5), :, lanes] = jnp.where(mask, value, jnp.zeros((5, 16, 128), BF16))
            ACC[...] += lax.dot_general(
                LHS[...].reshape(480, 2048), RHS[c].reshape(256, 2048), (((1,), (1,)), ((), ())),
                preferred_element_type=F32,
            )
            return 0

        lax.fori_loop(0, 8, add, 0)

        for i in range(3):
            for p in range(2):
                at = i * 160 + p * 40
                PUSH[i, p] = 0.5 * (ACC[at:at + 40, :] + ACC[at + 80:at + 120, :])
        push = pltpu.make_async_copy(PUSH, push_out, out_sem.at[2])
        push.start()
        push.wait()

    for d in range(8):
        if d:
            a2[d].wait_send()
            for k in range(CHUNKS):
                nf_copy(d, k).wait_send()
            e2_copy(d).wait_send()
        a3_copy(d).wait_send()
        e1_copy(d).wait_send()
    for pair in pairs + v_edges + [pr_x, pr_y, p1_x, p1_y, p2_x, p2_y]:
        for copy in pair:
            copy.wait_send()
    f1_sends(lambda copy: copy.wait_send())
    for copy in outs:
        copy.wait()


def finish_kernel(ov, p2, push_in, vel_out, pres_out, WV, WP, PUSH, load_sem, out_sem):
    slab = lax.axis_index("slab")
    cross = lax.axis_index("cross")

    def straight(k, lo, n):
        return [
            pltpu.make_async_copy(ov.at[:, pl.ds(lo, n)], vel_out.at[:, pl.ds(lo, n)], out_sem.at[2 * k]),
            pltpu.make_async_copy(p2.at[pl.ds(lo, n)], pres_out.at[pl.ds(lo, n)], out_sem.at[2 * k + 1]),
        ]

    def run(first, lo):
        if first is not None:
            loads = [
                pltpu.make_async_copy(push_in, PUSH, load_sem.at[0]),
                pltpu.make_async_copy(ov.at[:, pl.ds(lo, 4)], WV, load_sem.at[1]),
                pltpu.make_async_copy(p2.at[pl.ds(lo, 4)], WP, load_sem.at[2]),
            ]
            for load in loads:
                load.start()
        if first is None:
            copies = straight(0, 0, 16)
        else:
            copies = straight(0, 4 - lo // 3, 12)
        for copy in copies:
            copy.start()
        if first is not None:
            for load in loads:
                load.wait()
            correct(first, cross, PUSH, WV, WP)
            late = [
                pltpu.make_async_copy(WV, vel_out.at[:, pl.ds(lo, 4)], out_sem.at[2]),
                pltpu.make_async_copy(WP, pres_out.at[pl.ds(lo, 4)], out_sem.at[3]),
            ]
            for copy in late:
                copy.start()
            copies = copies + late
        for copy in copies:
            copy.wait()

    @pl.when(slab == 7)
    def _():
        run(124, 12)

    @pl.when(slab == 8)
    def _():
        run(128, 0)

    @pl.when((slab != 7) & (slab != 8))
    def _():
        run(None, 0)


def correct(first, cross, PUSH, WV, WP):
    push = {(i, 127 + p): PUSH[i, p] for i in range(3) for p in range(2)}
    row = lax.broadcasted_iota(jnp.int32, (40, 256), 0) + (cross * 32 - 4)
    inside = (row >= 0) & (row < 256)

    def within(a):
        return jnp.where(inside, a, 0.0)

    def ny(a):
        return pltpu.roll(a, 39, 0)

    def py(a):
        return pltpu.roll(a, 1, 0)

    div = {126: 0.5 * push[0, 127], 129: -0.5 * push[0, 128]}
    for x, side in ((127, push[0, 128]), (128, -push[0, 127])):
        a, b = push[1, x], push[2, x]
        div[x] = within(0.5 * (side + (ny(a) - py(a)) + (z_next(b) - z_prev(b))))
    one = {x: -SIXTH * div[x] for x in div}
    two = {}
    for x in range(125, 131):
        s = None
        if x in one:
            a = one[x]
            s = ny(a) + py(a) + z_next(a) + z_prev(a) - div[x]
        for near in (x - 1, x + 1):
            if near in one:
                s = one[near] if s is None else s + one[near]
        two[x] = within(s * SIXTH)

    def centre(a):
        return pltpu.roll(a, 36, 0)[0:32]

    def apply(first):
        for n in range(4):
            x = first + n
            g = None
            if x + 1 in two:
                g = two[x + 1]
            if x - 1 in two:
                g = -two[x - 1] if g is None else g - two[x - 1]
            vx = -0.5 * g
            if x in (127, 128):
                vx = vx + push[0, x]
            WV[0, n] += centre(vx)
            if x in two:
                a = two[x]
                WP[n] += centre(a)
                vy = -0.5 * (ny(a) - py(a))
                vz = -0.5 * (z_next(a) - z_prev(a))
                if x in (127, 128):
                    vy = vy + push[1, x]
                    vz = vz + push[2, x]
                WV[1, n] += centre(vy)
                WV[2, n] += centre(vz)

    apply(first)


def body(velocity, pressure, inv_influence, normals, sample_cells, tangents, force_owner, force_cell):
    any_space = pl.BlockSpec(memory_space=pl.ANY)
    dma = pltpu.SemaphoreType.DMA
    vm = pltpu.VMEM
    ov, p2, push = pl.pallas_call(
        kernel,
        out_shape=(
            jax.ShapeDtypeStruct(velocity.shape, F32),
            jax.ShapeDtypeStruct(pressure.shape, F32),
            jax.ShapeDtypeStruct((3, 2, 40, 256), F32),
        ),
        in_specs=[any_space] * 8,
        out_specs=(any_space,) * 3,
        scratch_shapes=[
            vm((3, 18, 32, 256), F32), vm((18, 32, 256), F32), vm((3, 18, 32, 256), F32),
            vm((18, 32, 256), F32), vm((18, 32, 256), F32), vm((16, 32, 256), F32), vm((3, 16, 32, 256), F32),
            vm((7, 2, 16, 256), F32), vm((7, 2, 16, 256), F32),
            vm((3, 256, 256), F32), vm((384, 512), BF16), vm((8, 2, 128, 1024), BF16), vm((128, 256), jnp.int32),
            vm((128, 256), F32), vm((128, 256), F32), vm((128, 256), jnp.int32),
            pltpu.SMEM((3, 128), F32), vm((3, 1, 1, 128), F32),
            vm((128, 128), jnp.int32), vm((128, 128), jnp.int32), vm((128, 128), F32), vm((128, 128), F32),
            vm((128, 256), F32), vm((8, 128, 256), F32), vm((8, 128, 256), BF16),
            vm((8, 128, 256), F32), vm((8, 128, 256), F32), vm((8, 128, 256), F32), vm((8, 128, 256), F32),
            vm((3, 128), F32), vm((8, 16, 3, 128), F32),
            vm((30, 16, 2048), BF16), vm((8, 16, 16, 2048), BF16), vm((480, 256), F32), vm((3, 2, 40, 256), F32),
            dma((8,)), dma((1,)), dma((16,)), dma((1,)), dma((8,)), dma((8,)), dma((8,)), dma((8,)),
            dma((8, CHUNKS)), dma((8, CHUNKS)), dma((8,)), dma((8,)), dma((8,)), dma((8,)),
            dma((16,)), dma((1,)), dma((5, 2)), dma((5, 2)), dma((7, 2)), dma((7, 2)),
            dma((3,)),
        ],
        compiler_params=pltpu.CompilerParams(
            collective_id=0, has_side_effects=True, vmem_limit_bytes=56 * 1024 * 1024
        ),
    )(
        velocity, pressure, inv_influence.reshape(8, 2, 128, 1024),
        normals.reshape(3, 8, 128).transpose(1, 0, 2), sample_cells, tangents,
        force_owner.reshape(128, 128), force_cell.reshape(128, 128),
    )
    return pl.pallas_call(
        finish_kernel,
        out_shape=(
            jax.ShapeDtypeStruct(velocity.shape, F32),
            jax.ShapeDtypeStruct(pressure.shape, F32),
        ),
        in_specs=[any_space] * 3,
        out_specs=(any_space,) * 2,
        scratch_shapes=[
            vm((3, 4, 32, 256), F32), vm((4, 32, 256), F32), vm((3, 2, 40, 256), F32), dma((3,)), dma((4,)),
        ],
        compiler_params=pltpu.CompilerParams(vmem_limit_bytes=16 * 1024 * 1024),
    )(ov, p2, push)


def solution(mesh):
    return jax.shard_map(
        body,
        mesh=mesh,
        in_specs=(
            P(None, "slab", "cross", None),
            P("slab", "cross", None),
            P("cross", "slab"),
            P(None, "slab"),
            P("slab", None),
            P(None, "cross", "slab", None),
            P(),
            P(),
        ),
        out_specs=(P(None, "slab", "cross", None), P("slab", "cross", None)),
        check_vma=False,
    )
```

```python
import functools

import jax
import jax.numpy as jnp
from jax import lax
from jax.experimental import pallas as pl
from jax.experimental.pallas import tpu as pltpu
from jax.sharding import PartitionSpec as P

MESH = pl.DeviceIdType.MESH
F32 = jnp.float32
BF16 = jnp.bfloat16
SIXTH = 1.0 / 6.0
GROUP = 16


def z_next(a):
    lane = lax.broadcasted_iota(jnp.int32, a.shape, 1)
    return jnp.where(lane == 255, 0.0, pltpu.roll(a, 255, 1))


def z_prev(a):
    lane = lax.broadcasted_iota(jnp.int32, a.shape, 1)
    return jnp.where(lane == 0, 0.0, pltpu.roll(a, 1, 1))


def y_next(a, edge):
    n = a.shape[0]
    row = lax.broadcasted_iota(jnp.int32, a.shape, 0)
    return jnp.where(row == n - 1, edge, pltpu.roll(a, n - 1, 0))


def y_prev(a, edge):
    n = a.shape[0]
    row = lax.broadcasted_iota(jnp.int32, a.shape, 0)
    return jnp.where(row == 0, edge, pltpu.roll(a, 1, 0))


def kernel(
    vel, pres, inv, nrm, cells, tang, owner, cell,
    ov_out, p2_out, push_out,
    V, P0, PR, P1, P2, DV, OV,
    EDGE_S, EDGE_R,
    PL, T, A, CI, ZB, YH, YL, NS, TG, KO, KC, RK, ZK,
    NFS, NF, NFB, SB, RB1, RB2, FB, FA, LHS, RHS, ACC, PUSH, PUSH2,
    load_sem, ns_sem, a1s, a1r, a2s, a2r, a3s, a3r, ns, nr, e1s, e1r, e2s, e2r,
    f1s, f1r, f2s, f2r, xs, xr, ys, yr, out_sem,
):
    slab = lax.axis_index("slab")
    cross = lax.axis_index("cross")
    h = lax.rem(slab, 2)
    chip = slab // 2
    sib = slab + 1 - 2 * h

    def remote(src, dst, ss, rs, s, c):
        return pltpu.make_async_remote_copy(
            src_ref=src, dst_ref=dst, send_sem=ss, recv_sem=rs, device_id=(s, c), device_id_type=MESH
        )

    def cr(d):
        return lax.rem(cross + d, 8)

    def sl(d):
        return lax.rem(slab + d, 16)

    loads = [
        pltpu.make_async_copy(vel, V.at[:, pl.ds(1, 16)], load_sem.at[0]),
        pltpu.make_async_copy(pres, P0.at[pl.ds(1, 16)], load_sem.at[1]),
        pltpu.make_async_copy(cells.at[pl.ds(pl.multiple_of(cross * 128, 128), 128)], CI, load_sem.at[2]),
        pltpu.make_async_copy(nrm.at[cross], NS, load_sem.at[3]),
        pltpu.make_async_copy(inv.at[:, 0], A.at[0], load_sem.at[4]),
        pltpu.make_async_copy(tang, TG, load_sem.at[5]),
        pltpu.make_async_copy(owner, KO, load_sem.at[6]),
        pltpu.make_async_copy(cell, KC, load_sem.at[7]),
        pltpu.make_async_copy(inv.at[:, 1], A.at[1], load_sem.at[8]),
    ]
    for n in (0, 1, 2, 3, 5, 6, 7):
        loads[n].start()

    barrier = pltpu.get_barrier_semaphore()
    for d in range(1, 16):
        pl.semaphore_signal(barrier, inc=1, device_id=(sl(d), cross), device_id_type=MESH)
    for d in range(1, 8):
        pl.semaphore_signal(barrier, inc=1, device_id=(slab, cr(d)), device_id_type=MESH)
    pl.semaphore_wait(barrier, 22)

    def a1_copy(target, k):
        half = target % 2
        return remote(
            vel.at[k, 8, pl.ds(half * 16, 16)],
            PL.at[k, pl.ds(pl.multiple_of(cross * 32 + half * 16, 16), 16)],
            a1s.at[k, target], a1r.at[k], target, cross,
        )

    def tile(c, half, k):
        return PL.at[k, pl.ds(pl.multiple_of(c * 32 + half * 16, 16), 16)]

    others = [t for t in (6, 8, 5, 4, 9, 2, 1, 3, 0, 10, 14, 15, 11, 13, 12)]

    @pl.when(slab == 7)
    def _():
        for k in range(3):
            pltpu.make_async_copy(vel.at[k, 8, pl.ds(16, 16)], tile(cross, 1, k), a1r.at[k]).start()
            for t in others:
                a1_copy(t, k).start()

    def x_pair(src_hi, dst_lo, src_lo, dst_hi, k):
        up = remote(src_hi, dst_lo, xs.at[k, 0], xr.at[k, 0], sl(1), cross)
        down = remote(src_lo, dst_hi, xs.at[k, 1], xr.at[k, 1], sl(15), cross)
        return up, down

    def y_pair(k):
        up = remote(EDGE_S.at[k, 0], EDGE_R.at[k, 0], ys.at[k, 0], yr.at[k, 0], slab, cr(1))
        down = remote(EDGE_S.at[k, 1], EDGE_R.at[k, 1], ys.at[k, 1], yr.at[k, 1], slab, cr(7))
        return up, down

    pairs = [x_pair(vel.at[:, 15], V.at[:, 0], vel.at[:, 0], V.at[:, 17], 0),
             x_pair(pres.at[15], P0.at[0], pres.at[0], P0.at[17], 1)]
    for pair in pairs:
        for copy in pair:
            copy.start()

    loads[0].wait()
    loads[1].wait()

    def fill_edges(k, source):
        def step(x, _):
            EDGE_S[k, 0, pl.ds(x, 1), :] = source(x, 31)
            EDGE_S[k, 1, pl.ds(x, 1), :] = source(x, 0)
            return 0
        lax.fori_loop(0, 16, step, 0)

    for i in range(3):
        fill_edges(i, lambda x, r, i=i: V[i, x + 1, r:r + 1, :])
    fill_edges(3, lambda x, r: P0[x + 1, r:r + 1, :])
    v_edges = [y_pair(k) for k in range(4)]
    for pair in v_edges:
        for copy in pair:
            copy.start()

    def finish(pair):
        for copy in pair:
            copy.wait_recv()

    def clear_planes(refs):
        @pl.when(slab == 0)
        def _():
            for ref, lo, hi in refs:
                lo[...] = jnp.zeros(lo.shape, F32)

        @pl.when(slab == 15)
        def _():
            for ref, lo, hi in refs:
                hi[...] = jnp.zeros(hi.shape, F32)

    def clear_rows(ks):
        @pl.when(cross == 0)
        def _():
            for k in ks:
                EDGE_R[k, 0] = jnp.zeros((16, 256), F32)

        @pl.when(cross == 7)
        def _():
            for k in ks:
                EDGE_R[k, 1] = jnp.zeros((16, 256), F32)

    loads[2].wait()
    for q in range(2):
        for n in range(2):
            ci = CI[n * 64:(n + 1) * 64, q * 128:(q + 1) * 128]
            side = slice(n * 128, (n + 1) * 128)
            ZB[q, :, side] = (ci & 255).astype(F32)
            YH[q, :, side] = (ci >> 15).astype(F32)
            YL[q, :, side] = (ci >> 8) & 127

    loads[6].wait()
    loads[7].wait()
    ko = KO[...]
    kc = KC[...]
    rel = (ko & 7) * 32 + (kc >> 8) - (cross * 32 - 4)
    RK[...] = jnp.where((rel >= 0) & (rel < 40), (ko >> 3) * 40 + rel, -1).astype(F32)
    ZK[...] = (kc & 255).astype(F32)

    def place_all():
        z_at = (lax.broadcasted_iota(jnp.int32, (16, 16, 128), 0) * 16
                + lax.broadcasted_iota(jnp.int32, (16, 16, 128), 1)).astype(F32).astype(BF16)

        def place(c, _):
            for s in range(16):
                zk = jnp.broadcast_to(ZK[pl.ds((h * 4 + c) * 16 + s, 1), :], (16, 128)).astype(BF16)[None]
                RHS[c, :, :, s * 128:(s + 1) * 128] = jnp.where(
                    z_at == zk, jnp.ones((1, 16, 128), BF16), jnp.zeros((16, 16, 128), BF16)
                )
            return 0
        lax.fori_loop(0, 4, place, 0)

    @pl.when((slab == 8) | (slab == 9))
    def _():
        place_all()

    def a2_copy(d, k):
        return remote(tile(cross, h, k), tile(cross, h, k), a2s.at[k, d], a2r.at[k, d], slab, cr(d))

    def a3_copy(d, k):
        src = tile(cr(8 - d), h, k)
        return remote(src, src, a3s.at[k, d], a3r.at[k, d], sib, cross)

    for k in range(3):
        remote(vel.at[k, 8, pl.ds(0, 16)], tile(cross, h, k), a1s.at[k, 0], a1r.at[k], slab, cross).wait_recv()
        for d in (4, 1, 7, 3, 5, 2, 6):
            a2_copy(d, k).start()
        a3_copy(0, k).start()

    loads[4].start()
    loads[8].start()

    @pl.when((slab == 6) | (slab == 7))
    def _():
        place_all()

    for pair in pairs:
        finish(pair)
    for pair in v_edges:
        finish(pair)
    clear_planes([(V, V.at[:, 0], V.at[:, 17]), (P0, P0.at[0], P0.at[17])])
    clear_rows(range(4))

    def around(u, lo, hi, k, x):
        mid = u(x + 1)
        s = u(x + 2) + u(x)
        s = s + y_next(mid, EDGE_R[k, 1, pl.ds(x, 1), :]) + y_prev(mid, EDGE_R[k, 0, pl.ds(x, 1), :])
        return s + z_next(mid) + z_prev(mid)

    def predict(x, _):
        for i in range(3):
            mid = V[i, x + 1]
            s = around(lambda q: V[i, q], None, None, i, x)
            pr = mid + 0.5 * (0.1 * (s - 6.0 * mid))
            PR[i, x + 1] = pr
            if i == 1:
                EDGE_S[4, 0, pl.ds(x, 1), :] = pr[31:32, :]
                EDGE_S[4, 1, pl.ds(x, 1), :] = pr[0:1, :]
        return 0

    lax.fori_loop(0, 16, predict, 0)
    pr_x = x_pair(PR.at[0, 16], PR.at[0, 0], PR.at[0, 1], PR.at[0, 17], 2)
    pr_y = y_pair(4)
    for copy in pr_x + pr_y:
        copy.start()

    for k in range(3):
        for d in (1, 7, 4, 3, 5, 2, 6):
            remote(tile(cross, h, k), tile(cr(8 - d), h, k), a2s.at[k, d], a2r.at[k, d], slab, cross).wait_recv()
            a3_copy(d, k).start()

    for k in range(3):
        for d in (0, 1, 7, 4, 3, 5, 2, 6):
            remote(tile(cross, h, k), tile(cr(8 - d), 1 - h, k), a3s.at[k, d], a3r.at[k, d], sib, cross).wait_recv()
    for c in range(3):
        for k in range(2):
            T[pl.ds(c * 128, 128), pl.ds(k * 256, 256)] = PL[c, pl.ds(k * 128, 128), :].astype(BF16)

    loads[3].wait()

    row16 = lax.broadcasted_iota(jnp.int32, (16, 16, 256), 0) * 16 + lax.broadcasted_iota(jnp.int32, (16, 16, 256), 1)
    z_of = row16.astype(F32).astype(BF16)
    y_of = lax.broadcasted_iota(jnp.int32, (16, 8, 256), 0) * 8 + lax.broadcasted_iota(jnp.int32, (16, 8, 256), 1)

    def lookup(q, m):
        zb = jnp.broadcast_to(ZB[q, pl.ds(m, 1), :], (16, 256)).astype(BF16)[None]
        yh = jnp.broadcast_to(YH[q, pl.ds(m, 1), :], (16, 256)).astype(BF16)[None]
        mask = z_of == zb
        zero = jnp.zeros((16, 16, 256), BF16)
        one = jnp.ones((1, 16, 256), BF16)
        hot = jnp.concatenate(
            [jnp.where(mask, one - yh, zero).reshape(256, 256), jnp.where(mask, yh, zero).reshape(256, 256)], axis=0
        )
        r = jnp.dot(T[...], hot, preferred_element_type=F32).reshape(3, 16, 8, 256)
        ym = y_of == jnp.broadcast_to(YL[q, pl.ds(m, 1), :], (8, 256))[None]
        a = [jnp.sum(jnp.where(ym, r[i], 0.0), axis=0) for i in range(3)]
        for n in range(2):
            side = slice(n * 128, (n + 1) * 128)
            j = n * 64 + m
            acc = NS[0, j] * a[0][:, side] + NS[1, j] * a[1][:, side] + NS[2, j] * a[2][:, side]
            NFS[q, n, pl.ds(m, 1), :] = jnp.sum(acc, axis=0, keepdims=True).astype(BF16).astype(F32)

    def nf_copy(q, d, part):
        return remote(NFS.at[q, :, part], NF.at[q, cross, :, part], ns.at[q, d], nr.at[q, d], slab, cr(d))

    def nf_wait(q):
        NFB[q, cross] = NFS[q].reshape(128, 128).astype(BF16)

        def take(d, _):
            src = cr(8 - d)
            remote(NFS.at[q], NF.at[q, src], ns.at[q, d], nr.at[q, d], slab, cross).wait_recv()
            NFB[q, src] = NF[q, src].reshape(128, 128).astype(BF16)
            return 0
        lax.fori_loop(1, 8, take, 0)

    def at(d):
        return lax.rem(chip + d, 8)

    def e1_copy(q, d):
        return remote(SB.at[q, 0, at(d)], RB1.at[q, at(d)], e1s.at[q, d], e1r.at[q, d], sib, cross)

    def e2_copy(q, d):
        return remote(SB.at[q, 1, at(d)], RB2.at[q, d], e2s.at[q, d], e2r.at[q, d], at(d) * 2 + h, cross)

    def e1_start(q):
        def part(t, _):
            half = lax.rem(h + 1 + t, 2)
            out = jnp.dot(A[half].reshape(1024, 1024), NFB[q].reshape(1024, 128), preferred_element_type=F32)
            SB[q, t] = out.reshape(8, 128, 128)

            @pl.when(t == 0)
            def _():
                for d in (1, 2, 3, 4, 5, 6, 7, 0):
                    e1_copy(q, d).start()
            return 0
        lax.fori_loop(0, 2, part, 0)

    def e2_start(q):
        for d in (1, 2, 3, 4, 5, 6, 7, 0):
            e1_copy(q, d).wait_recv()
            SB[q, 1, at(d)] += RB1[q, at(d)]
            if d:
                e2_copy(q, d).start()

    p1_x = x_pair(P1.at[16], P1.at[0], P1.at[1], P1.at[17], 3)
    p1_y = y_pair(5)

    def diverge_all():
        finish(pr_x)
        finish(pr_y)
        clear_planes([(PR, PR.at[0, 0], PR.at[0, 17])])
        clear_rows([4])

        def diverge(x, _):
            py = PR[1, x + 1]
            pz = PR[2, x + 1]
            g = PR[0, x + 2] - PR[0, x]
            g = g + (y_next(py, EDGE_R[4, 1, pl.ds(x, 1), :]) - y_prev(py, EDGE_R[4, 0, pl.ds(x, 1), :]))
            g = 0.5 * (g + (z_next(pz) - z_prev(pz)))
            DV[x] = g
            p = (around(lambda q: P0[q], None, None, 3, x) - g) * SIXTH
            P1[x + 1] = p
            EDGE_S[5, 0, pl.ds(x, 1), :] = p[31:32, :]
            EDGE_S[5, 1, pl.ds(x, 1), :] = p[0:1, :]
            return 0

        lax.fori_loop(0, 16, diverge, 0)
        for copy in p1_x + p1_y:
            copy.start()

    loads[4].wait()
    loads[8].wait()

    def step(it, _):
        q = it // 4
        first = lax.rem(it, 4) * GROUP

        @pl.when(it < 8)
        def _():
            for g in range(GROUP):
                lookup(q, first + g)
            for d in (4, 1, 7, 3, 5, 2, 6):
                nf_copy(q, d, pl.ds(pl.multiple_of(first, GROUP), GROUP)).start()

        @pl.when(it == 8)
        def _():
            diverge_all()

        @pl.when((it == 6) | (it == 8))
        def _():
            late = (it - 6) // 2
            nf_wait(late)
            e1_start(late)

        @pl.when(it == 7)
        def _():
            e2_start(0)
        return 0

    lax.fori_loop(0, 9, step, 0)
    e2_start(1)

    finish(p1_x)
    finish(p1_y)
    clear_planes([(P1, P1.at[0], P1.at[17])])
    clear_rows([5])

    def sweep(x, _):
        p = (around(lambda q: P1[q], None, None, 5, x) - DV[x]) * SIXTH
        P2[x + 1] = p
        EDGE_S[6, 0, pl.ds(x, 1), :] = p[31:32, :]
        EDGE_S[6, 1, pl.ds(x, 1), :] = p[0:1, :]
        return 0

    lax.fori_loop(0, 16, sweep, 0)
    p2_x = x_pair(P2.at[16], P2.at[0], P2.at[1], P2.at[17], 4)
    p2_y = y_pair(6)
    for copy in p2_x + p2_y:
        copy.start()

    finish(p2_x)
    finish(p2_y)
    clear_planes([(P2, P2.at[0], P2.at[17])])
    clear_rows([6])

    def correct(x, _):
        mid = P2[x + 1]
        OV[0, x] = PR[0, x + 1] - 0.5 * (P2[x + 2] - P2[x])
        gy = y_next(mid, EDGE_R[6, 1, pl.ds(x, 1), :]) - y_prev(mid, EDGE_R[6, 0, pl.ds(x, 1), :])
        OV[1, x] = PR[1, x + 1] - 0.5 * gy
        OV[2, x] = PR[2, x + 1] - 0.5 * (z_next(mid) - z_prev(mid))
        return 0

    lax.fori_loop(0, 16, correct, 0)

    outs = [
        pltpu.make_async_copy(OV, ov_out, out_sem.at[0]),
        pltpu.make_async_copy(P2.at[pl.ds(1, 16)], p2_out, out_sem.at[1]),
    ]
    for copy in outs:
        copy.start()

    loads[5].wait()
    square = None
    for q in range(2):
        total = SB[q, 1, chip]
        for d in range(1, 8):
            e2_copy(q, d).wait_recv()
            total = total + RB2[q, d]
        square = total * total if square is None else square + total * total
    mean = lax.dot_general(
        jnp.ones((8, 128), F32), square, (((1,), (1,)), ((), ())),
        precision=lax.Precision.HIGHEST, preferred_element_type=F32,
    )[0:1] * (1.0 / 256.0)
    FB[...] = TG[:, 0, 0, :] * mean

    side = cross // 4
    slot = lax.rem(cross, 4)

    def f1_copy(n, d):
        return remote(FB, FA.at[slot, slab], f1s.at[n * 8 + d], f1r.at[0], 6 + 2 * n + side, cr(d))

    def f1_sends(act):
        for d in (4, 2, 6, 3, 5, 1, 7, 0):
            for n in range(2):
                if d:
                    act(f1_copy(n, d))
                else:
                    @pl.when(slab != 6 + 2 * n + side)
                    def _():
                        act(f1_copy(n, 0))

    f1_sends(lambda copy: copy.start())

    @pl.when((slab >= 6) & (slab <= 9))
    def _():
        @pl.when(side == h)
        def _():
            pltpu.make_async_copy(FB, FA.at[slot, slab], f1r.at[0]).start()

        remote(FA, FA, f1s.at[0], f1r.at[0], slab, cross).wait_recv()

        r_of = (lax.broadcasted_iota(jnp.int32, (5, 16, 128), 0) * 16
                + lax.broadcasted_iota(jnp.int32, (5, 16, 128), 1)).astype(F32).astype(BF16)
        ACC[...] = jnp.zeros(ACC.shape, F32)

        def add(c, _):
            for s in range(16):
                q = (h * 4 + c) * 16 + s
                lanes = pl.ds(s * 128, 128)
                rk = jnp.broadcast_to(RK[pl.ds(q, 1), :], (16, 128)).astype(BF16)[None]
                f = FA[c, s]
                hi = f.astype(BF16).astype(F32)
                lo = f - hi
                mask = r_of == rk
                for i in range(3):
                    for n, part in enumerate((hi, lo)):
                        value = jnp.broadcast_to(part[i:i + 1], (16, 128)).astype(BF16)[None]
                        LHS[pl.ds((i * 2 + n) * 5, 5), :, lanes] = jnp.where(mask, value, jnp.zeros((5, 16, 128), BF16))
            ACC[...] += lax.dot_general(
                LHS[...].reshape(480, 2048), RHS[c].reshape(256, 2048), (((1,), (1,)), ((), ())),
                preferred_element_type=F32,
            )
            return 0

        lax.fori_loop(0, 4, add, 0)

        for i in range(3):
            for p in range(2):
                at = i * 160 + p * 40
                PUSH[i, p] = 0.5 * (ACC[at:at + 40, :] + ACC[at + 80:at + 120, :])
        share = remote(PUSH, PUSH2, f2s.at[0], f2r.at[0], sib, cross)

        @pl.when((slab == 6) | (slab == 9))
        def _():
            share.start()
            share.wait_send()

        @pl.when((slab == 7) | (slab == 8))
        def _():
            share.wait_recv()
            PUSH[...] += PUSH2[...]
            push = pltpu.make_async_copy(PUSH, push_out, out_sem.at[2])
            push.start()
            push.wait()

    @pl.when(slab == 7)
    def _():
        for k in range(3):
            for t in others:
                a1_copy(t, k).wait_send()
    for d in range(8):
        for k in range(3):
            if d:
                a2_copy(d, k).wait_send()
            a3_copy(d, k).wait_send()
        for q in range(2):
            if d:
                remote(NFS.at[q], NF.at[q, cross], ns.at[q, d], nr.at[q, d], slab, cr(d)).wait_send()
                e2_copy(q, d).wait_send()
            e1_copy(q, d).wait_send()
    for pair in pairs + v_edges + [pr_x, pr_y, p1_x, p1_y, p2_x, p2_y]:
        for copy in pair:
            copy.wait_send()
    f1_sends(lambda copy: copy.wait_send())
    for copy in outs:
        copy.wait()


def finish_kernel(ov, p2, push_in, vel_out, pres_out, WV, WP, PUSH, load_sem, out_sem):
    slab = lax.axis_index("slab")
    cross = lax.axis_index("cross")

    def moves(k, into):
        part = pl.ds(4 * k, 4)
        if into:
            return [
                pltpu.make_async_copy(ov.at[:, part], WV.at[:, part], load_sem.at[k]),
                pltpu.make_async_copy(p2.at[part], WP.at[part], load_sem.at[4 + k]),
            ]
        return [
            pltpu.make_async_copy(WV.at[:, part], vel_out.at[:, part], out_sem.at[k]),
            pltpu.make_async_copy(WP.at[part], pres_out.at[part], out_sem.at[4 + k]),
        ]

    def run(first, last):
        if first is not None:
            load = pltpu.make_async_copy(push_in, PUSH, load_sem.at[8])
            load.start()
        order = [k for k in range(4) if k != last] + [last]
        for k in [last] + order[:3]:
            for copy in moves(k, True):
                copy.start()
        for k in order:
            for copy in moves(k, True):
                copy.wait()
            if k == last and first is not None:
                load.wait()
                correct(first, 4 * k, cross, PUSH, WV, WP)
            for copy in moves(k, False):
                copy.start()
        for k in range(4):
            for copy in moves(k, False):
                copy.wait()

    @pl.when(slab == 7)
    def _():
        run(124, 3)

    @pl.when(slab == 8)
    def _():
        run(128, 0)

    @pl.when((slab != 7) & (slab != 8))
    def _():
        run(None, 3)


def correct(first, at, cross, PUSH, WV, WP):
    push = {(i, 127 + p): PUSH[i, p] for i in range(3) for p in range(2)}
    row = lax.broadcasted_iota(jnp.int32, (40, 256), 0) + (cross * 32 - 4)
    inside = (row >= 0) & (row < 256)

    def within(a):
        return jnp.where(inside, a, 0.0)

    def ny(a):
        return pltpu.roll(a, 39, 0)

    def py(a):
        return pltpu.roll(a, 1, 0)

    div = {126: 0.5 * push[0, 127], 129: -0.5 * push[0, 128]}
    for x, side in ((127, push[0, 128]), (128, -push[0, 127])):
        a, b = push[1, x], push[2, x]
        div[x] = within(0.5 * (side + (ny(a) - py(a)) + (z_next(b) - z_prev(b))))
    one = {x: -SIXTH * div[x] for x in div}
    two = {}
    for x in range(125, 131):
        s = None
        if x in one:
            a = one[x]
            s = ny(a) + py(a) + z_next(a) + z_prev(a) - div[x]
        for near in (x - 1, x + 1):
            if near in one:
                s = one[near] if s is None else s + one[near]
        two[x] = within(s * SIXTH)

    def centre(a):
        return pltpu.roll(a, 36, 0)[0:32]

    def apply(first):
        for n in range(4):
            x = first + n
            g = None
            if x + 1 in two:
                g = two[x + 1]
            if x - 1 in two:
                g = -two[x - 1] if g is None else g - two[x - 1]
            vx = -0.5 * g
            if x in (127, 128):
                vx = vx + push[0, x]
            WV[0, at + n] += centre(vx)
            if x in two:
                a = two[x]
                WP[at + n] += centre(a)
                vy = -0.5 * (ny(a) - py(a))
                vz = -0.5 * (z_next(a) - z_prev(a))
                if x in (127, 128):
                    vy = vy + push[1, x]
                    vz = vz + push[2, x]
                WV[1, at + n] += centre(vy)
                WV[2, at + n] += centre(vz)

    apply(first)


def body(velocity, pressure, inv_influence, normals, sample_cells, tangents, force_owner, force_cell):
    any_space = pl.BlockSpec(memory_space=pl.ANY)
    dma = pltpu.SemaphoreType.DMA
    vm = pltpu.VMEM
    ov, p2, push = pl.pallas_call(
        kernel,
        out_shape=(
            jax.ShapeDtypeStruct(velocity.shape, F32),
            jax.ShapeDtypeStruct(pressure.shape, F32),
            jax.ShapeDtypeStruct((3, 2, 40, 256), F32),
        ),
        in_specs=[any_space] * 8,
        out_specs=(any_space,) * 3,
        scratch_shapes=[
            vm((3, 18, 32, 256), F32), vm((18, 32, 256), F32), vm((3, 18, 32, 256), F32),
            vm((18, 32, 256), F32), vm((18, 32, 256), F32), vm((16, 32, 256), F32), vm((3, 16, 32, 256), F32),
            vm((7, 2, 16, 256), F32), vm((7, 2, 16, 256), F32),
            vm((3, 256, 256), F32), vm((384, 512), BF16), vm((2, 8, 128, 1024), BF16), vm((128, 256), jnp.int32),
            vm((2, 64, 256), F32), vm((2, 64, 256), F32), vm((2, 64, 256), jnp.int32),
            pltpu.SMEM((3, 128), F32), vm((3, 1, 1, 128), F32),
            vm((128, 128), jnp.int32), vm((128, 128), jnp.int32), vm((128, 128), F32), vm((128, 128), F32),
            vm((2, 2, 64, 128), F32), vm((2, 8, 2, 64, 128), F32), vm((2, 8, 128, 128), BF16),
            vm((2, 2, 8, 128, 128), F32), vm((2, 8, 128, 128), F32), vm((2, 8, 128, 128), F32),
            vm((3, 128), F32), vm((4, 16, 3, 128), F32),
            vm((30, 16, 2048), BF16), vm((4, 16, 16, 2048), BF16), vm((480, 256), F32), vm((3, 2, 40, 256), F32), vm((3, 2, 40, 256), F32),
            dma((9,)), dma((1,)), dma((3, 16)), dma((3,)), dma((3, 8)), dma((3, 8)), dma((3, 8)), dma((3, 8)),
            dma((2, 8)), dma((2, 8)), dma((2, 8)), dma((2, 8)), dma((2, 8)), dma((2, 8)),
            dma((16,)), dma((1,)), dma((1,)), dma((1,)), dma((5, 2)), dma((5, 2)), dma((7, 2)), dma((7, 2)),
            dma((3,)),
        ],
        compiler_params=pltpu.CompilerParams(
            collective_id=0, has_side_effects=True, vmem_limit_bytes=56 * 1024 * 1024
        ),
    )(
        velocity, pressure, inv_influence.reshape(8, 2, 128, 1024),
        normals.reshape(3, 8, 128).transpose(1, 0, 2), sample_cells, tangents,
        force_owner.reshape(128, 128), force_cell.reshape(128, 128),
    )
    return pl.pallas_call(
        finish_kernel,
        out_shape=(
            jax.ShapeDtypeStruct(velocity.shape, F32),
            jax.ShapeDtypeStruct(pressure.shape, F32),
        ),
        in_specs=[any_space] * 3,
        out_specs=(any_space,) * 2,
        scratch_shapes=[
            vm((3, 16, 32, 256), F32), vm((16, 32, 256), F32), vm((3, 2, 40, 256), F32), dma((9,)), dma((8,)),
        ],
        compiler_params=pltpu.CompilerParams(vmem_limit_bytes=56 * 1024 * 1024),
    )(ov, p2, push)


def solution(mesh):
    return jax.shard_map(
        body,
        mesh=mesh,
        in_specs=(
            P(None, "slab", "cross", None),
            P("slab", "cross", None),
            P("cross", "slab"),
            P(None, "slab"),
            P("slab", None),
            P(None, "cross", "slab", None),
            P(),
            P(),
        ),
        out_specs=(P(None, "slab", "cross", None), P("slab", "cross", None)),
        check_vma=False,
    )
```

```python
import functools

import jax
import jax.numpy as jnp
from jax import lax
from jax.experimental import pallas as pl
from jax.experimental.pallas import tpu as pltpu
from jax.sharding import PartitionSpec as P

MESH = pl.DeviceIdType.MESH
F32 = jnp.float32
BF16 = jnp.bfloat16
SIXTH = 1.0 / 6.0
GROUP = 16


def z_next(a):
    lane = lax.broadcasted_iota(jnp.int32, a.shape, 1)
    return jnp.where(lane == 255, 0.0, pltpu.roll(a, 255, 1))


def z_prev(a):
    lane = lax.broadcasted_iota(jnp.int32, a.shape, 1)
    return jnp.where(lane == 0, 0.0, pltpu.roll(a, 1, 1))


def y_next(a, edge):
    n = a.shape[0]
    row = lax.broadcasted_iota(jnp.int32, a.shape, 0)
    return jnp.where(row == n - 1, edge, pltpu.roll(a, n - 1, 0))


def y_prev(a, edge):
    n = a.shape[0]
    row = lax.broadcasted_iota(jnp.int32, a.shape, 0)
    return jnp.where(row == 0, edge, pltpu.roll(a, 1, 0))


def kernel(
    vel, pres, inv, nrm, cells, tang, owner, cell,
    ov_out, p2_out, push_out,
    V, P0, PR, P1, P2, DV, OV,
    EDGE_S, EDGE_R,
    PL, T, A, CI, ZB, YH, YL, NS, TG, KO, KC, RK, ZK,
    NFS, NF, NFB, SB, RB1, RB2, FB, FA, LHS, RHS, ACC, PUSH, PUSH2,
    load_sem, ns_sem, a1s, a1r, a2s, a2r, a3s, a3r, ns, nr, e1s, e1r, e2s, e2r,
    f1s, f1r, f2s, f2r, xs, xr, ys, yr, out_sem,
):
    slab = lax.axis_index("slab")
    cross = lax.axis_index("cross")
    h = lax.rem(slab, 2)
    chip = slab // 2
    sib = slab + 1 - 2 * h

    def remote(src, dst, ss, rs, s, c):
        return pltpu.make_async_remote_copy(
            src_ref=src, dst_ref=dst, send_sem=ss, recv_sem=rs, device_id=(s, c), device_id_type=MESH
        )

    def cr(d):
        return lax.rem(cross + d, 8)

    def sl(d):
        return lax.rem(slab + d, 16)

    loads = [
        pltpu.make_async_copy(vel, V.at[:, pl.ds(1, 16)], load_sem.at[0]),
        pltpu.make_async_copy(pres, P0.at[pl.ds(1, 16)], load_sem.at[1]),
        pltpu.make_async_copy(cells.at[pl.ds(pl.multiple_of(cross * 128, 128), 128)], CI, load_sem.at[2]),
        pltpu.make_async_copy(nrm.at[cross], NS, load_sem.at[3]),
        pltpu.make_async_copy(inv.at[:, 0], A.at[0], load_sem.at[4]),
        pltpu.make_async_copy(tang, TG, load_sem.at[5]),
        pltpu.make_async_copy(owner, KO, load_sem.at[6]),
        pltpu.make_async_copy(cell, KC, load_sem.at[7]),
        pltpu.make_async_copy(inv.at[:, 1], A.at[1], load_sem.at[8]),
    ]
    for n in (0, 1, 2, 3, 5, 6, 7):
        loads[n].start()

    barrier = pltpu.get_barrier_semaphore()
    for d in range(1, 16):
        pl.semaphore_signal(barrier, inc=1, device_id=(sl(d), cross), device_id_type=MESH)
    for d in range(1, 8):
        pl.semaphore_signal(barrier, inc=1, device_id=(slab, cr(d)), device_id_type=MESH)
    pl.semaphore_wait(barrier, 22)

    def a1_copy(target, k):
        half = target % 2
        return remote(
            vel.at[k, 8, pl.ds(half * 16, 16)],
            PL.at[k, pl.ds(pl.multiple_of(cross * 32 + half * 16, 16), 16)],
            a1s.at[k, target], a1r.at[k], target, cross,
        )

    def tile(c, half, k):
        return PL.at[k, pl.ds(pl.multiple_of(c * 32 + half * 16, 16), 16)]

    others = [t for t in (6, 8, 5, 4, 9, 2, 1, 3, 0, 10, 14, 15, 11, 13, 12)]

    @pl.when(slab == 7)
    def _():
        for k in range(3):
            pltpu.make_async_copy(vel.at[k, 8, pl.ds(16, 16)], tile(cross, 1, k), a1r.at[k]).start()
            for t in others:
                a1_copy(t, k).start()

    def x_pair(src_hi, dst_lo, src_lo, dst_hi, k):
        up = remote(src_hi, dst_lo, xs.at[k, 0], xr.at[k, 0], sl(1), cross)
        down = remote(src_lo, dst_hi, xs.at[k, 1], xr.at[k, 1], sl(15), cross)
        return up, down

    def y_pair(k):
        up = remote(EDGE_S.at[k, 0], EDGE_R.at[k, 0], ys.at[k, 0], yr.at[k, 0], slab, cr(1))
        down = remote(EDGE_S.at[k, 1], EDGE_R.at[k, 1], ys.at[k, 1], yr.at[k, 1], slab, cr(7))
        return up, down

    pairs = [x_pair(vel.at[:, 15], V.at[:, 0], vel.at[:, 0], V.at[:, 17], 0),
             x_pair(pres.at[15], P0.at[0], pres.at[0], P0.at[17], 1)]
    def fill_edges(k, source):
        def step(x, _):
            EDGE_S[k, 0, pl.ds(x, 1), :] = source(x, 31)
            EDGE_S[k, 1, pl.ds(x, 1), :] = source(x, 0)
            return 0
        lax.fori_loop(0, 16, step, 0)

    def finish(pair):
        for copy in pair:
            copy.wait_recv()

    def clear_planes(refs):
        @pl.when(slab == 0)
        def _():
            for ref, lo, hi in refs:
                lo[...] = jnp.zeros(lo.shape, F32)

        @pl.when(slab == 15)
        def _():
            for ref, lo, hi in refs:
                hi[...] = jnp.zeros(hi.shape, F32)

    def clear_rows(ks):
        @pl.when(cross == 0)
        def _():
            for k in ks:
                EDGE_R[k, 0] = jnp.zeros((16, 256), F32)

        @pl.when(cross == 7)
        def _():
            for k in ks:
                EDGE_R[k, 1] = jnp.zeros((16, 256), F32)

    loads[2].wait()
    for q in range(2):
        for n in range(2):
            ci = CI[n * 64:(n + 1) * 64, q * 128:(q + 1) * 128]
            side = slice(n * 128, (n + 1) * 128)
            ZB[q, :, side] = (ci & 255).astype(F32)
            YH[q, :, side] = (ci >> 15).astype(F32)
            YL[q, :, side] = (ci >> 8) & 127

    loads[6].wait()
    loads[7].wait()
    ko = KO[...]
    kc = KC[...]
    rel = (ko & 7) * 32 + (kc >> 8) - (cross * 32 - 4)
    RK[...] = jnp.where((rel >= 0) & (rel < 40), (ko >> 3) * 40 + rel, -1).astype(F32)
    ZK[...] = (kc & 255).astype(F32)

    def place_all():
        z_at = (lax.broadcasted_iota(jnp.int32, (16, 16, 128), 0) * 16
                + lax.broadcasted_iota(jnp.int32, (16, 16, 128), 1)).astype(F32).astype(BF16)

        def place(c, _):
            for s in range(16):
                zk = jnp.broadcast_to(ZK[pl.ds((h * 4 + c) * 16 + s, 1), :], (16, 128)).astype(BF16)[None]
                RHS[c, :, :, s * 128:(s + 1) * 128] = jnp.where(
                    z_at == zk, jnp.ones((1, 16, 128), BF16), jnp.zeros((16, 16, 128), BF16)
                )
            return 0
        lax.fori_loop(0, 4, place, 0)

    @pl.when((slab == 8) | (slab == 9))
    def _():
        place_all()

    def a2_copy(d, k):
        return remote(tile(cross, h, k), tile(cross, h, k), a2s.at[k, d], a2r.at[k, d], slab, cr(d))

    def a3_copy(d, k):
        src = tile(cr(8 - d), h, k)
        return remote(src, src, a3s.at[k, d], a3r.at[k, d], sib, cross)

    for k in range(3):
        remote(vel.at[k, 8, pl.ds(0, 16)], tile(cross, h, k), a1s.at[k, 0], a1r.at[k], slab, cross).wait_recv()
        for d in (4, 1, 7, 3, 5, 2, 6):
            a2_copy(d, k).start()
        a3_copy(0, k).start()

    loads[4].start()
    loads[8].start()

    @pl.when((slab == 6) | (slab == 7))
    def _():
        place_all()

    loads[0].wait()
    loads[1].wait()
    for i in range(3):
        fill_edges(i, lambda x, r, i=i: V[i, x + 1, r:r + 1, :])
    fill_edges(3, lambda x, r: P0[x + 1, r:r + 1, :])
    v_edges = [y_pair(k) for k in range(4)]
    for pair in v_edges:
        for copy in pair:
            copy.start()
    for pair in pairs:
        for copy in pair:
            copy.start()

    for k in range(3):
        for d in (1, 7, 4, 3, 5, 2, 6):
            remote(tile(cross, h, k), tile(cr(8 - d), h, k), a2s.at[k, d], a2r.at[k, d], slab, cross).wait_recv()
            a3_copy(d, k).start()

    for k in range(3):
        for d in (0, 1, 7, 4, 3, 5, 2, 6):
            remote(tile(cross, h, k), tile(cr(8 - d), 1 - h, k), a3s.at[k, d], a3r.at[k, d], sib, cross).wait_recv()
    for c in range(3):
        for k in range(2):
            T[pl.ds(c * 128, 128), pl.ds(k * 256, 256)] = PL[c, pl.ds(k * 128, 128), :].astype(BF16)

    loads[3].wait()

    row16 = lax.broadcasted_iota(jnp.int32, (16, 16, 256), 0) * 16 + lax.broadcasted_iota(jnp.int32, (16, 16, 256), 1)
    z_of = row16.astype(F32).astype(BF16)
    y_of = lax.broadcasted_iota(jnp.int32, (16, 8, 256), 0) * 8 + lax.broadcasted_iota(jnp.int32, (16, 8, 256), 1)

    def lookup(q, m):
        zb = jnp.broadcast_to(ZB[q, pl.ds(m, 1), :], (16, 256)).astype(BF16)[None]
        yh = jnp.broadcast_to(YH[q, pl.ds(m, 1), :], (16, 256)).astype(BF16)[None]
        mask = z_of == zb
        zero = jnp.zeros((16, 16, 256), BF16)
        one = jnp.ones((1, 16, 256), BF16)
        hot = jnp.concatenate(
            [jnp.where(mask, one - yh, zero).reshape(256, 256), jnp.where(mask, yh, zero).reshape(256, 256)], axis=0
        )
        r = jnp.dot(T[...], hot, preferred_element_type=F32).reshape(3, 16, 8, 256)
        ym = y_of == jnp.broadcast_to(YL[q, pl.ds(m, 1), :], (8, 256))[None]
        a = [jnp.sum(jnp.where(ym, r[i], 0.0), axis=0) for i in range(3)]
        for n in range(2):
            side = slice(n * 128, (n + 1) * 128)
            j = n * 64 + m
            acc = NS[0, j] * a[0][:, side] + NS[1, j] * a[1][:, side] + NS[2, j] * a[2][:, side]
            NFS[q, n, pl.ds(m, 1), :] = jnp.sum(acc, axis=0, keepdims=True).astype(BF16).astype(F32)

    def nf_copy(q, d, part):
        return remote(NFS.at[q, :, part], NF.at[q, cross, :, part], ns.at[q, d], nr.at[q, d], slab, cr(d))

    def nf_wait(q):
        NFB[q, cross] = NFS[q].reshape(128, 128).astype(BF16)

        def take(d, _):
            src = cr(8 - d)
            remote(NFS.at[q], NF.at[q, src], ns.at[q, d], nr.at[q, d], slab, cross).wait_recv()
            NFB[q, src] = NF[q, src].reshape(128, 128).astype(BF16)
            return 0
        lax.fori_loop(1, 8, take, 0)

    def at(d):
        return lax.rem(chip + d, 8)

    def e1_copy(q, d):
        return remote(SB.at[q, 0, at(d)], RB1.at[q, at(d)], e1s.at[q, d], e1r.at[q, d], sib, cross)

    def e2_copy(q, d):
        return remote(SB.at[q, 1, at(d)], RB2.at[q, d], e2s.at[q, d], e2r.at[q, d], at(d) * 2 + h, cross)

    def e1_start(q):
        def part(t, _):
            half = lax.rem(h + 1 + t, 2)
            out = jnp.dot(A[half].reshape(1024, 1024), NFB[q].reshape(1024, 128), preferred_element_type=F32)
            SB[q, t] = out.reshape(8, 128, 128)

            @pl.when(t == 0)
            def _():
                for d in (6, 4, 2, 5, 7, 1, 3, 0):
                    e1_copy(q, d).start()
            return 0
        lax.fori_loop(0, 2, part, 0)

    def e2_start(q):
        for d in (6, 4, 2, 5, 7, 1, 3, 0):
            e1_copy(q, d).wait_recv()
            SB[q, 1, at(d)] += RB1[q, at(d)]
            if d:
                e2_copy(q, d).start()

    def around(u, lo, hi, k, x):
        mid = u(x + 1)
        s = u(x + 2) + u(x)
        s = s + y_next(mid, EDGE_R[k, 1, pl.ds(x, 1), :]) + y_prev(mid, EDGE_R[k, 0, pl.ds(x, 1), :])
        return s + z_next(mid) + z_prev(mid)

    def predict(x, _):
        for i in range(3):
            mid = V[i, x + 1]
            s = around(lambda q: V[i, q], None, None, i, x)
            pr = mid + 0.5 * (0.1 * (s - 6.0 * mid))
            PR[i, x + 1] = pr
            if i == 1:
                EDGE_S[4, 0, pl.ds(x, 1), :] = pr[31:32, :]
                EDGE_S[4, 1, pl.ds(x, 1), :] = pr[0:1, :]
        return 0

    pr_x = x_pair(PR.at[0, 16], PR.at[0, 0], PR.at[0, 1], PR.at[0, 17], 2)
    pr_y = y_pair(4)

    def predict_all():
        for pair in pairs:
            finish(pair)
        for pair in v_edges:
            finish(pair)
        clear_planes([(V, V.at[:, 0], V.at[:, 17]), (P0, P0.at[0], P0.at[17])])
        clear_rows(range(4))

        lax.fori_loop(0, 16, predict, 0)
        for copy in pr_x + pr_y:
            copy.start()

    p1_x = x_pair(P1.at[16], P1.at[0], P1.at[1], P1.at[17], 3)
    p1_y = y_pair(5)

    def diverge_all():
        finish(pr_x)
        finish(pr_y)
        clear_planes([(PR, PR.at[0, 0], PR.at[0, 17])])
        clear_rows([4])

        def diverge(x, _):
            py = PR[1, x + 1]
            pz = PR[2, x + 1]
            g = PR[0, x + 2] - PR[0, x]
            g = g + (y_next(py, EDGE_R[4, 1, pl.ds(x, 1), :]) - y_prev(py, EDGE_R[4, 0, pl.ds(x, 1), :]))
            g = 0.5 * (g + (z_next(pz) - z_prev(pz)))
            DV[x] = g
            p = (around(lambda q: P0[q], None, None, 3, x) - g) * SIXTH
            P1[x + 1] = p
            EDGE_S[5, 0, pl.ds(x, 1), :] = p[31:32, :]
            EDGE_S[5, 1, pl.ds(x, 1), :] = p[0:1, :]
            return 0

        lax.fori_loop(0, 16, diverge, 0)
        for copy in p1_x + p1_y:
            copy.start()

    loads[4].wait()
    loads[8].wait()

    def step(it, _):
        q = it // 4
        first = lax.rem(it, 4) * GROUP

        @pl.when(it < 8)
        def _():
            for g in range(GROUP):
                lookup(q, first + g)
            for d in (4, 1, 7, 3, 5, 2, 6):
                nf_copy(q, d, pl.ds(pl.multiple_of(first, GROUP), GROUP)).start()

        @pl.when(it == 8)
        def _():
            e2_start(0)
            predict_all()

        @pl.when((it == 7) | (it == 8))
        def _():
            late = it - 7
            nf_wait(late)
            e1_start(late)

        return 0

    lax.fori_loop(0, 9, step, 0)
    e2_start(1)
    diverge_all()

    loads[5].wait()
    square = None
    for q in range(2):
        total = SB[q, 1, chip]
        for d in range(1, 8):
            e2_copy(q, d).wait_recv()
            total = total + RB2[q, d]
        square = total * total if square is None else square + total * total
    mean = lax.dot_general(
        jnp.ones((8, 128), F32), square, (((1,), (1,)), ((), ())),
        precision=lax.Precision.HIGHEST, preferred_element_type=F32,
    )[0:1] * (1.0 / 256.0)
    FB[...] = TG[:, 0, 0, :] * mean

    side = cross // 4
    slot = lax.rem(cross, 4)

    def f1_copy(n, d):
        return remote(FB, FA.at[slot, slab], f1s.at[n * 8 + d], f1r.at[0], 6 + 2 * n + side, cr(d))

    def f1_sends(act):
        for d in (4, 2, 6, 3, 5, 1, 7, 0):
            for n in range(2):
                if d:
                    act(f1_copy(n, d))
                else:
                    @pl.when(slab != 6 + 2 * n + side)
                    def _():
                        act(f1_copy(n, 0))

    f1_sends(lambda copy: copy.start())

    finish(p1_x)
    finish(p1_y)
    clear_planes([(P1, P1.at[0], P1.at[17])])
    clear_rows([5])

    def sweep(x, _):
        p = (around(lambda q: P1[q], None, None, 5, x) - DV[x]) * SIXTH
        P2[x + 1] = p
        EDGE_S[6, 0, pl.ds(x, 1), :] = p[31:32, :]
        EDGE_S[6, 1, pl.ds(x, 1), :] = p[0:1, :]
        return 0

    lax.fori_loop(0, 16, sweep, 0)
    p2_x = x_pair(P2.at[16], P2.at[0], P2.at[1], P2.at[17], 4)
    p2_y = y_pair(6)
    for copy in p2_x + p2_y:
        copy.start()

    finish(p2_x)
    finish(p2_y)
    clear_planes([(P2, P2.at[0], P2.at[17])])
    clear_rows([6])

    def correct(x, _):
        mid = P2[x + 1]
        OV[0, x] = PR[0, x + 1] - 0.5 * (P2[x + 2] - P2[x])
        gy = y_next(mid, EDGE_R[6, 1, pl.ds(x, 1), :]) - y_prev(mid, EDGE_R[6, 0, pl.ds(x, 1), :])
        OV[1, x] = PR[1, x + 1] - 0.5 * gy
        OV[2, x] = PR[2, x + 1] - 0.5 * (z_next(mid) - z_prev(mid))
        return 0

    lax.fori_loop(0, 16, correct, 0)

    outs = [
        pltpu.make_async_copy(OV, ov_out, out_sem.at[0]),
        pltpu.make_async_copy(P2.at[pl.ds(1, 16)], p2_out, out_sem.at[1]),
    ]
    for copy in outs:
        copy.start()

    @pl.when((slab >= 6) & (slab <= 9))
    def _():
        @pl.when(side == h)
        def _():
            pltpu.make_async_copy(FB, FA.at[slot, slab], f1r.at[0]).start()

        remote(FA, FA, f1s.at[0], f1r.at[0], slab, cross).wait_recv()

        r_of = (lax.broadcasted_iota(jnp.int32, (5, 16, 128), 0) * 16
                + lax.broadcasted_iota(jnp.int32, (5, 16, 128), 1)).astype(F32).astype(BF16)
        ACC[...] = jnp.zeros(ACC.shape, F32)

        def add(c, _):
            for s in range(16):
                q = (h * 4 + c) * 16 + s
                lanes = pl.ds(s * 128, 128)
                rk = jnp.broadcast_to(RK[pl.ds(q, 1), :], (16, 128)).astype(BF16)[None]
                f = FA[c, s]
                hi = f.astype(BF16).astype(F32)
                lo = f - hi
                mask = r_of == rk
                for i in range(3):
                    for n, part in enumerate((hi, lo)):
                        value = jnp.broadcast_to(part[i:i + 1], (16, 128)).astype(BF16)[None]
                        LHS[pl.ds((i * 2 + n) * 5, 5), :, lanes] = jnp.where(mask, value, jnp.zeros((5, 16, 128), BF16))
            ACC[...] += lax.dot_general(
                LHS[...].reshape(480, 2048), RHS[c].reshape(256, 2048), (((1,), (1,)), ((), ())),
                preferred_element_type=F32,
            )
            return 0

        lax.fori_loop(0, 4, add, 0)

        for i in range(3):
            for p in range(2):
                at = i * 160 + p * 40
                PUSH[i, p] = 0.5 * (ACC[at:at + 40, :] + ACC[at + 80:at + 120, :])
        share = remote(PUSH, PUSH2, f2s.at[0], f2r.at[0], sib, cross)

        @pl.when((slab == 6) | (slab == 9))
        def _():
            share.start()
            share.wait_send()

        @pl.when((slab == 7) | (slab == 8))
        def _():
            share.wait_recv()
            PUSH[...] += PUSH2[...]
            push = pltpu.make_async_copy(PUSH, push_out, out_sem.at[2])
            push.start()
            push.wait()

    @pl.when(slab == 7)
    def _():
        for k in range(3):
            for t in others:
                a1_copy(t, k).wait_send()
    for d in range(8):
        for k in range(3):
            if d:
                a2_copy(d, k).wait_send()
            a3_copy(d, k).wait_send()
        for q in range(2):
            if d:
                remote(NFS.at[q], NF.at[q, cross], ns.at[q, d], nr.at[q, d], slab, cr(d)).wait_send()
                e2_copy(q, d).wait_send()
            e1_copy(q, d).wait_send()
    for pair in pairs + v_edges + [pr_x, pr_y, p1_x, p1_y, p2_x, p2_y]:
        for copy in pair:
            copy.wait_send()
    f1_sends(lambda copy: copy.wait_send())
    for copy in outs:
        copy.wait()


def finish_kernel(ov, p2, push_in, vel_out, pres_out, WV, WP, PUSH, load_sem, out_sem):
    slab = lax.axis_index("slab")
    cross = lax.axis_index("cross")

    def moves(k, into):
        part = pl.ds(4 * k, 4)
        if into:
            return [
                pltpu.make_async_copy(ov.at[:, part], WV.at[:, part], load_sem.at[k]),
                pltpu.make_async_copy(p2.at[part], WP.at[part], load_sem.at[4 + k]),
            ]
        return [
            pltpu.make_async_copy(WV.at[:, part], vel_out.at[:, part], out_sem.at[k]),
            pltpu.make_async_copy(WP.at[part], pres_out.at[part], out_sem.at[4 + k]),
        ]

    def run(first, last):
        if first is not None:
            load = pltpu.make_async_copy(push_in, PUSH, load_sem.at[8])
            load.start()
        order = [k for k in range(4) if k != last] + [last]
        for k in [last] + order[:3]:
            for copy in moves(k, True):
                copy.start()
        for k in order:
            for copy in moves(k, True):
                copy.wait()
            if k == last and first is not None:
                load.wait()
                correct(first, 4 * k, cross, PUSH, WV, WP)
            for copy in moves(k, False):
                copy.start()
        for k in range(4):
            for copy in moves(k, False):
                copy.wait()

    @pl.when(slab == 7)
    def _():
        run(124, 3)

    @pl.when(slab == 8)
    def _():
        run(128, 0)

    @pl.when((slab != 7) & (slab != 8))
    def _():
        run(None, 3)


def correct(first, at, cross, PUSH, WV, WP):
    push = {(i, 127 + p): PUSH[i, p] for i in range(3) for p in range(2)}
    row = lax.broadcasted_iota(jnp.int32, (40, 256), 0) + (cross * 32 - 4)
    inside = (row >= 0) & (row < 256)

    def within(a):
        return jnp.where(inside, a, 0.0)

    def ny(a):
        return pltpu.roll(a, 39, 0)

    def py(a):
        return pltpu.roll(a, 1, 0)

    div = {126: 0.5 * push[0, 127], 129: -0.5 * push[0, 128]}
    for x, side in ((127, push[0, 128]), (128, -push[0, 127])):
        a, b = push[1, x], push[2, x]
        div[x] = within(0.5 * (side + (ny(a) - py(a)) + (z_next(b) - z_prev(b))))
    one = {x: -SIXTH * div[x] for x in div}
    two = {}
    for x in range(125, 131):
        s = None
        if x in one:
            a = one[x]
            s = ny(a) + py(a) + z_next(a) + z_prev(a) - div[x]
        for near in (x - 1, x + 1):
            if near in one:
                s = one[near] if s is None else s + one[near]
        two[x] = within(s * SIXTH)

    def centre(a):
        return pltpu.roll(a, 36, 0)[0:32]

    def apply(first):
        for n in range(4):
            x = first + n
            g = None
            if x + 1 in two:
                g = two[x + 1]
            if x - 1 in two:
                g = -two[x - 1] if g is None else g - two[x - 1]
            vx = -0.5 * g
            if x in (127, 128):
                vx = vx + push[0, x]
            WV[0, at + n] += centre(vx)
            if x in two:
                a = two[x]
                WP[at + n] += centre(a)
                vy = -0.5 * (ny(a) - py(a))
                vz = -0.5 * (z_next(a) - z_prev(a))
                if x in (127, 128):
                    vy = vy + push[1, x]
                    vz = vz + push[2, x]
                WV[1, at + n] += centre(vy)
                WV[2, at + n] += centre(vz)

    apply(first)


def body(velocity, pressure, inv_influence, normals, sample_cells, tangents, force_owner, force_cell):
    any_space = pl.BlockSpec(memory_space=pl.ANY)
    dma = pltpu.SemaphoreType.DMA
    vm = pltpu.VMEM
    ov, p2, push = pl.pallas_call(
        kernel,
        out_shape=(
            jax.ShapeDtypeStruct(velocity.shape, F32),
            jax.ShapeDtypeStruct(pressure.shape, F32),
            jax.ShapeDtypeStruct((3, 2, 40, 256), F32),
        ),
        in_specs=[any_space] * 8,
        out_specs=(any_space,) * 3,
        scratch_shapes=[
            vm((3, 18, 32, 256), F32), vm((18, 32, 256), F32), vm((3, 18, 32, 256), F32),
            vm((18, 32, 256), F32), vm((18, 32, 256), F32), vm((16, 32, 256), F32), vm((3, 16, 32, 256), F32),
            vm((7, 2, 16, 256), F32), vm((7, 2, 16, 256), F32),
            vm((3, 256, 256), F32), vm((384, 512), BF16), vm((2, 8, 128, 1024), BF16), vm((128, 256), jnp.int32),
            vm((2, 64, 256), F32), vm((2, 64, 256), F32), vm((2, 64, 256), jnp.int32),
            pltpu.SMEM((3, 128), F32), vm((3, 1, 1, 128), F32),
            vm((128, 128), jnp.int32), vm((128, 128), jnp.int32), vm((128, 128), F32), vm((128, 128), F32),
            vm((2, 2, 64, 128), F32), vm((2, 8, 2, 64, 128), F32), vm((2, 8, 128, 128), BF16),
            vm((2, 2, 8, 128, 128), F32), vm((2, 8, 128, 128), F32), vm((2, 8, 128, 128), F32),
            vm((3, 128), F32), vm((4, 16, 3, 128), F32),
            vm((30, 16, 2048), BF16), vm((4, 16, 16, 2048), BF16), vm((480, 256), F32), vm((3, 2, 40, 256), F32), vm((3, 2, 40, 256), F32),
            dma((9,)), dma((1,)), dma((3, 16)), dma((3,)), dma((3, 8)), dma((3, 8)), dma((3, 8)), dma((3, 8)),
            dma((2, 8)), dma((2, 8)), dma((2, 8)), dma((2, 8)), dma((2, 8)), dma((2, 8)),
            dma((16,)), dma((1,)), dma((1,)), dma((1,)), dma((5, 2)), dma((5, 2)), dma((7, 2)), dma((7, 2)),
            dma((3,)),
        ],
        compiler_params=pltpu.CompilerParams(
            collective_id=0, has_side_effects=True, vmem_limit_bytes=56 * 1024 * 1024
        ),
    )(
        velocity, pressure, inv_influence.reshape(8, 2, 128, 1024),
        normals.reshape(3, 8, 128).transpose(1, 0, 2), sample_cells, tangents,
        force_owner.reshape(128, 128), force_cell.reshape(128, 128),
    )
    return pl.pallas_call(
        finish_kernel,
        out_shape=(
            jax.ShapeDtypeStruct(velocity.shape, F32),
            jax.ShapeDtypeStruct(pressure.shape, F32),
        ),
        in_specs=[any_space] * 3,
        out_specs=(any_space,) * 2,
        scratch_shapes=[
            vm((3, 16, 32, 256), F32), vm((16, 32, 256), F32), vm((3, 2, 40, 256), F32), dma((9,)), dma((8,)),
        ],
        compiler_params=pltpu.CompilerParams(vmem_limit_bytes=56 * 1024 * 1024),
    )(ov, p2, push)


def solution(mesh):
    return jax.shard_map(
        body,
        mesh=mesh,
        in_specs=(
            P(None, "slab", "cross", None),
            P("slab", "cross", None),
            P("cross", "slab"),
            P(None, "slab"),
            P("slab", None),
            P(None, "cross", "slab", None),
            P(),
            P(),
        ),
        out_specs=(P(None, "slab", "cross", None), P("slab", "cross", None)),
        check_vma=False,
    )
```

```python
import functools

import jax
import jax.numpy as jnp
from jax import lax
from jax.experimental import pallas as pl
from jax.experimental.pallas import tpu as pltpu
from jax.sharding import PartitionSpec as P

MESH = pl.DeviceIdType.MESH
F32 = jnp.float32
BF16 = jnp.bfloat16
SIXTH = 1.0 / 6.0
GROUP = 32
PARTS = 64 // GROUP


def z_next(a):
    lane = lax.broadcasted_iota(jnp.int32, a.shape, 1)
    return jnp.where(lane == 255, 0.0, pltpu.roll(a, 255, 1))


def z_prev(a):
    lane = lax.broadcasted_iota(jnp.int32, a.shape, 1)
    return jnp.where(lane == 0, 0.0, pltpu.roll(a, 1, 1))


def y_next(a, edge):
    n = a.shape[0]
    row = lax.broadcasted_iota(jnp.int32, a.shape, 0)
    return jnp.where(row == n - 1, edge, pltpu.roll(a, n - 1, 0))


def y_prev(a, edge):
    n = a.shape[0]
    row = lax.broadcasted_iota(jnp.int32, a.shape, 0)
    return jnp.where(row == 0, edge, pltpu.roll(a, 1, 0))


def kernel(
    vel, pres, inv, nrm, cells, tang, owner, cell,
    ov_out, p2_out, push_out,
    V, P0, PR, P1, P2, DV, OV,
    EDGE_S, EDGE_R,
    PL, T, A, CI, ZB, YH, YL, NS, TG, KO, KC, RK, ZK,
    NFS, NF, NFB, SB, RB1, RB2, FB, FA, LHS, RHS, ACC, PUSH, PUSH2,
    load_sem, ns_sem, a1s, a1r, a2s, a2r, a3s, a3r, ns, nr, e1s, e1r, e2s, e2r,
    f1s, f1r, f2s, f2r, xs, xr, ys, yr, out_sem,
):
    slab = lax.axis_index("slab")
    cross = lax.axis_index("cross")
    h = lax.rem(slab, 2)
    chip = slab // 2
    sib = slab + 1 - 2 * h

    def remote(src, dst, ss, rs, s, c):
        return pltpu.make_async_remote_copy(
            src_ref=src, dst_ref=dst, send_sem=ss, recv_sem=rs, device_id=(s, c), device_id_type=MESH
        )

    def cr(d):
        return lax.rem(cross + d, 8)

    def peer(d):
        return lax.rem(cross // 4 + d // 4, 2) * 4 + lax.rem(cross + d, 4)

    def peer_in(d):
        return lax.rem(cross // 4 + d // 4, 2) * 4 + lax.rem(cross + 8 - d, 4)

    def sl(d):
        return lax.rem(slab + d, 16)

    loads = [
        pltpu.make_async_copy(vel, V.at[:, pl.ds(1, 16)], load_sem.at[0]),
        pltpu.make_async_copy(pres, P0.at[pl.ds(1, 16)], load_sem.at[1]),
        pltpu.make_async_copy(cells.at[pl.ds(pl.multiple_of(cross * 128, 128), 128)], CI, load_sem.at[2]),
        pltpu.make_async_copy(nrm.at[cross], NS, load_sem.at[3]),
        pltpu.make_async_copy(inv.at[:, 0], A.at[0], load_sem.at[4]),
        pltpu.make_async_copy(tang, TG, load_sem.at[5]),
        pltpu.make_async_copy(owner, KO, load_sem.at[6]),
        pltpu.make_async_copy(cell, KC, load_sem.at[7]),
        pltpu.make_async_copy(inv.at[:, 1], A.at[1], load_sem.at[8]),
    ]
    for n in (0, 1, 2, 3, 5, 6, 7):
        loads[n].start()

    barrier = pltpu.get_barrier_semaphore()
    for d in range(1, 16):
        pl.semaphore_signal(barrier, inc=1, device_id=(sl(d), cross), device_id_type=MESH)
    for d in range(1, 8):
        pl.semaphore_signal(barrier, inc=1, device_id=(slab, cr(d)), device_id_type=MESH)
    pl.semaphore_wait(barrier, 22)

    def a1_copy(target, k):
        half = target % 2
        return remote(
            vel.at[k, 8, pl.ds(half * 16, 16)],
            PL.at[k, pl.ds(pl.multiple_of(cross * 32 + half * 16, 16), 16)],
            a1s.at[k, target], a1r.at[k], target, cross,
        )

    def tile(c, half, k):
        return PL.at[k, pl.ds(pl.multiple_of(c * 32 + half * 16, 16), 16)]

    others = [t for t in (6, 8, 5, 4, 9, 2, 1, 3, 0, 10, 14, 15, 11, 13, 12)]

    @pl.when(slab == 7)
    def _():
        for k in range(3):
            pltpu.make_async_copy(vel.at[k, 8, pl.ds(16, 16)], tile(cross, 1, k), a1r.at[k]).start()
            for t in others:
                a1_copy(t, k).start()

    def x_pair(src_hi, dst_lo, src_lo, dst_hi, k):
        up = remote(src_hi, dst_lo, xs.at[k, 0], xr.at[k, 0], sl(1), cross)
        down = remote(src_lo, dst_hi, xs.at[k, 1], xr.at[k, 1], sl(15), cross)
        return up, down

    def y_pair(k):
        up = remote(EDGE_S.at[k, 0], EDGE_R.at[k, 0], ys.at[k, 0], yr.at[k, 0], slab, cr(1))
        down = remote(EDGE_S.at[k, 1], EDGE_R.at[k, 1], ys.at[k, 1], yr.at[k, 1], slab, cr(7))
        return up, down

    pairs = [x_pair(vel.at[:, 15], V.at[:, 0], vel.at[:, 0], V.at[:, 17], 0),
             x_pair(pres.at[15], P0.at[0], pres.at[0], P0.at[17], 1)]
    def fill_edges(k, source):
        def step(x, _):
            EDGE_S[k, 0, pl.ds(x, 1), :] = source(x, 31)
            EDGE_S[k, 1, pl.ds(x, 1), :] = source(x, 0)
            return 0
        lax.fori_loop(0, 16, step, 0)

    def finish(pair):
        for copy in pair:
            copy.wait_recv()

    def clear_planes(refs):
        @pl.when(slab == 0)
        def _():
            for ref, lo, hi in refs:
                lo[...] = jnp.zeros(lo.shape, F32)

        @pl.when(slab == 15)
        def _():
            for ref, lo, hi in refs:
                hi[...] = jnp.zeros(hi.shape, F32)

    def clear_rows(ks):
        @pl.when(cross == 0)
        def _():
            for k in ks:
                EDGE_R[k, 0] = jnp.zeros((16, 256), F32)

        @pl.when(cross == 7)
        def _():
            for k in ks:
                EDGE_R[k, 1] = jnp.zeros((16, 256), F32)

    loads[2].wait()
    for q in range(2):
        for n in range(2):
            ci = CI[n * 64:(n + 1) * 64, q * 128:(q + 1) * 128]
            side = slice(n * 128, (n + 1) * 128)
            ZB[q, :, side] = (ci & 255).astype(F32)
            YH[q, :, side] = (ci >> 15).astype(F32)
            YL[q, :, side] = (ci >> 8) & 127

    loads[6].wait()
    loads[7].wait()
    ko = KO[...]
    kc = KC[...]
    rel = (ko & 7) * 32 + (kc >> 8) - (cross * 32 - 4)
    RK[...] = jnp.where((rel >= 0) & (rel < 40), (ko >> 3) * 40 + rel, -1).astype(F32)
    ZK[...] = (kc & 255).astype(F32)

    def place_all():
        z_at = (lax.broadcasted_iota(jnp.int32, (16, 16, 128), 0) * 16
                + lax.broadcasted_iota(jnp.int32, (16, 16, 128), 1)).astype(F32).astype(BF16)

        def place(c, _):
            for s in range(16):
                zk = jnp.broadcast_to(ZK[pl.ds((h * 4 + c) * 16 + s, 1), :], (16, 128)).astype(BF16)[None]
                RHS[c, :, :, s * 128:(s + 1) * 128] = jnp.where(
                    z_at == zk, jnp.ones((1, 16, 128), BF16), jnp.zeros((16, 16, 128), BF16)
                )
            return 0
        lax.fori_loop(0, 4, place, 0)

    @pl.when((slab == 8) | (slab == 9))
    def _():
        place_all()

    def a2_copy(d, k):
        return remote(tile(cross, h, k), tile(cross, h, k), a2s.at[k, d], a2r.at[k, d], slab, peer(d))

    def a3_copy(d, k):
        src = tile(peer_in(d), h, k)
        return remote(src, src, a3s.at[k, d], a3r.at[k, d], sib, cross)

    for k in range(3):
        remote(vel.at[k, 8, pl.ds(0, 16)], tile(cross, h, k), a1s.at[k, 0], a1r.at[k], slab, cross).wait_recv()
        for d in (6, 5, 7, 4, 2, 1, 3):
            a2_copy(d, k).start()
        a3_copy(0, k).start()

    loads[4].start()
    loads[8].start()

    @pl.when((slab == 6) | (slab == 7))
    def _():
        place_all()

    loads[0].wait()
    loads[1].wait()
    for i in range(3):
        fill_edges(i, lambda x, r, i=i: V[i, x + 1, r:r + 1, :])
    fill_edges(3, lambda x, r: P0[x + 1, r:r + 1, :])
    v_edges = [y_pair(k) for k in range(4)]
    for pair in v_edges:
        for copy in pair:
            copy.start()
    for pair in pairs:
        for copy in pair:
            copy.start()

    for k in range(3):
        for d in (1, 7, 4, 3, 5, 2, 6):
            remote(tile(cross, h, k), tile(peer_in(d), h, k), a2s.at[k, d], a2r.at[k, d], slab, cross).wait_recv()
            a3_copy(d, k).start()

    for k in range(3):
        for d in (0, 1, 7, 4, 3, 5, 2, 6):
            remote(tile(cross, h, k), tile(peer_in(d), 1 - h, k), a3s.at[k, d], a3r.at[k, d], sib, cross).wait_recv()
    for c in range(3):
        for k in range(2):
            T[pl.ds(c * 128, 128), pl.ds(k * 256, 256)] = PL[c, pl.ds(k * 128, 128), :].astype(BF16)

    loads[3].wait()

    row16 = lax.broadcasted_iota(jnp.int32, (16, 16, 256), 0) * 16 + lax.broadcasted_iota(jnp.int32, (16, 16, 256), 1)
    z_of = row16.astype(F32).astype(BF16)
    y_of = lax.broadcasted_iota(jnp.int32, (16, 8, 256), 0) * 8 + lax.broadcasted_iota(jnp.int32, (16, 8, 256), 1)

    def lookup(q, m):
        zb = jnp.broadcast_to(ZB[q, pl.ds(m, 1), :], (16, 256)).astype(BF16)[None]
        yh = jnp.broadcast_to(YH[q, pl.ds(m, 1), :], (16, 256)).astype(BF16)[None]
        mask = z_of == zb
        zero = jnp.zeros((16, 16, 256), BF16)
        one = jnp.ones((1, 16, 256), BF16)
        hot = jnp.concatenate(
            [jnp.where(mask, one - yh, zero).reshape(256, 256), jnp.where(mask, yh, zero).reshape(256, 256)], axis=0
        )
        r = jnp.dot(T[...], hot, preferred_element_type=F32).reshape(3, 16, 8, 256)
        ym = y_of == jnp.broadcast_to(YL[q, pl.ds(m, 1), :], (8, 256))[None]
        a = [jnp.sum(jnp.where(ym, r[i], 0.0), axis=0) for i in range(3)]
        for n in range(2):
            side = slice(n * 128, (n + 1) * 128)
            j = n * 64 + m
            acc = NS[0, j] * a[0][:, side] + NS[1, j] * a[1][:, side] + NS[2, j] * a[2][:, side]
            NFS[q, n, pl.ds(m, 1), :] = jnp.sum(acc, axis=0, keepdims=True).astype(BF16).astype(F32)

    def nf_copy(q, d, part):
        return remote(NFS.at[q, :, part], NF.at[q, cross, :, part], ns.at[q, d], nr.at[q, d], slab, peer(d))

    def nf_wait(q):
        NFB[q, cross] = NFS[q].reshape(128, 128).astype(BF16)

        def take(d, _):
            src = peer_in(d)
            remote(NFS.at[q], NF.at[q, src], ns.at[q, d], nr.at[q, d], slab, cross).wait_recv()
            NFB[q, src] = NF[q, src].reshape(128, 128).astype(BF16)
            return 0
        lax.fori_loop(1, 8, take, 0)

    def at(d):
        return lax.rem(chip // 4 + d // 4, 2) * 4 + lax.rem(chip + d, 4)

    def e1_copy(q, d):
        return remote(SB.at[q, 0, at(d)], RB1.at[q, at(d)], e1s.at[q, d], e1r.at[q, d], sib, cross)

    def e2_copy(q, d):
        return remote(SB.at[q, 1, at(d)], RB2.at[q, d], e2s.at[q, d], e2r.at[q, d], at(d) * 2 + h, cross)

    def e1_start(q):
        def part(t, _):
            half = lax.rem(h + 1 + t, 2)
            out = jnp.dot(A[half].reshape(1024, 1024), NFB[q].reshape(1024, 128), preferred_element_type=F32)
            SB[q, t] = out.reshape(8, 128, 128)

            @pl.when(t == 0)
            def _():
                for d in (6, 5, 7, 4, 2, 1, 3, 0):
                    e1_copy(q, d).start()
            return 0
        lax.fori_loop(0, 2, part, 0)

    def e2_start(q):
        for d in (6, 5, 7, 4, 2, 1, 3, 0):
            e1_copy(q, d).wait_recv()
            SB[q, 1, at(d)] += RB1[q, at(d)]
            if d:
                e2_copy(q, d).start()

    def around(u, lo, hi, k, x):
        mid = u(x + 1)
        s = u(x + 2) + u(x)
        s = s + y_next(mid, EDGE_R[k, 1, pl.ds(x, 1), :]) + y_prev(mid, EDGE_R[k, 0, pl.ds(x, 1), :])
        return s + z_next(mid) + z_prev(mid)

    def predict(x, _):
        for i in range(3):
            mid = V[i, x + 1]
            s = around(lambda q: V[i, q], None, None, i, x)
            pr = mid + 0.5 * (0.1 * (s - 6.0 * mid))
            PR[i, x + 1] = pr
            if i == 1:
                EDGE_S[4, 0, pl.ds(x, 1), :] = pr[31:32, :]
                EDGE_S[4, 1, pl.ds(x, 1), :] = pr[0:1, :]
        return 0

    pr_x = x_pair(PR.at[0, 16], PR.at[0, 0], PR.at[0, 1], PR.at[0, 17], 2)
    pr_y = y_pair(4)

    def predict_all():
        for pair in pairs:
            finish(pair)
        for pair in v_edges:
            finish(pair)
        clear_planes([(V, V.at[:, 0], V.at[:, 17]), (P0, P0.at[0], P0.at[17])])
        clear_rows(range(4))

        lax.fori_loop(0, 16, predict, 0)
        for copy in pr_x + pr_y:
            copy.start()

    p1_x = x_pair(P1.at[16], P1.at[0], P1.at[1], P1.at[17], 3)
    p1_y = y_pair(5)

    def diverge_all():
        finish(pr_x)
        finish(pr_y)
        clear_planes([(PR, PR.at[0, 0], PR.at[0, 17])])
        clear_rows([4])

        def diverge(x, _):
            py = PR[1, x + 1]
            pz = PR[2, x + 1]
            g = PR[0, x + 2] - PR[0, x]
            g = g + (y_next(py, EDGE_R[4, 1, pl.ds(x, 1), :]) - y_prev(py, EDGE_R[4, 0, pl.ds(x, 1), :]))
            g = 0.5 * (g + (z_next(pz) - z_prev(pz)))
            DV[x] = g
            p = (around(lambda q: P0[q], None, None, 3, x) - g) * SIXTH
            P1[x + 1] = p
            EDGE_S[5, 0, pl.ds(x, 1), :] = p[31:32, :]
            EDGE_S[5, 1, pl.ds(x, 1), :] = p[0:1, :]
            return 0

        lax.fori_loop(0, 16, diverge, 0)
        for copy in p1_x + p1_y:
            copy.start()

    loads[4].wait()
    loads[8].wait()

    def step(it, _):
        q = it // PARTS
        first = lax.rem(it, PARTS) * GROUP

        @pl.when(it < 2 * PARTS)
        def _():
            for g in range(GROUP):
                lookup(q, first + g)
            for d in (6, 5, 7, 4, 2, 1, 3):
                nf_copy(q, d, pl.ds(pl.multiple_of(first, GROUP), GROUP)).start()

        @pl.when(it == 2 * PARTS)
        def _():
            e2_start(0)
            predict_all()

        @pl.when(it >= 2 * PARTS - 1)
        def _():
            late = it - (2 * PARTS - 1)
            nf_wait(late)
            e1_start(late)

        return 0

    lax.fori_loop(0, 2 * PARTS + 1, step, 0)
    e2_start(1)
    diverge_all()

    @pl.when(slab == 7)
    def _():
        for k in range(3):
            for t in others:
                a1_copy(t, k).wait_send()
    for d in range(8):
        for k in range(3):
            if d:
                a2_copy(d, k).wait_send()
            a3_copy(d, k).wait_send()
        for q in range(2):
            if d:
                remote(NFS.at[q], NF.at[q, cross], ns.at[q, d], nr.at[q, d], slab, peer(d)).wait_send()
            e1_copy(q, d).wait_send()
    for pair in pairs + v_edges + [pr_x, pr_y]:
        for copy in pair:
            copy.wait_send()

    loads[5].wait()
    square = None
    for q in range(2):
        total = SB[q, 1, chip]
        for d in range(1, 8):
            e2_copy(q, d).wait_recv()
            total = total + RB2[q, d]
        square = total * total if square is None else square + total * total
    mean = lax.dot_general(
        jnp.ones((8, 128), F32), square, (((1,), (1,)), ((), ())),
        precision=lax.Precision.HIGHEST, preferred_element_type=F32,
    )[0:1] * (1.0 / 256.0)
    FB[...] = TG[:, 0, 0, :] * mean

    side = cross // 4
    slot = lax.rem(cross, 4)

    def f1_copy(n, d):
        return remote(FB, FA.at[slot, slab], f1s.at[n * 8 + d], f1r.at[0], 6 + 2 * n + side, cr(d))

    def f1_sends(act):
        for d in (4, 2, 6, 3, 5, 1, 7, 0):
            for n in range(2):
                if d:
                    act(f1_copy(n, d))
                else:
                    @pl.when(slab != 6 + 2 * n + side)
                    def _():
                        act(f1_copy(n, 0))

    f1_sends(lambda copy: copy.start())

    for q in range(2):
        for d in range(1, 8):
            e2_copy(q, d).wait_send()
    for copy in p1_x + p1_y:
        copy.wait_send()

    finish(p1_x)
    finish(p1_y)
    clear_planes([(P1, P1.at[0], P1.at[17])])
    clear_rows([5])

    def sweep(x, _):
        p = (around(lambda q: P1[q], None, None, 5, x) - DV[x]) * SIXTH
        P2[x + 1] = p
        EDGE_S[6, 0, pl.ds(x, 1), :] = p[31:32, :]
        EDGE_S[6, 1, pl.ds(x, 1), :] = p[0:1, :]
        return 0

    lax.fori_loop(0, 16, sweep, 0)
    p2_x = x_pair(P2.at[16], P2.at[0], P2.at[1], P2.at[17], 4)
    p2_y = y_pair(6)
    for copy in p2_x + p2_y:
        copy.start()

    finish(p2_x)
    finish(p2_y)
    clear_planes([(P2, P2.at[0], P2.at[17])])
    clear_rows([6])

    def correct(x, _):
        mid = P2[x + 1]
        OV[0, x] = PR[0, x + 1] - 0.5 * (P2[x + 2] - P2[x])
        gy = y_next(mid, EDGE_R[6, 1, pl.ds(x, 1), :]) - y_prev(mid, EDGE_R[6, 0, pl.ds(x, 1), :])
        OV[1, x] = PR[1, x + 1] - 0.5 * gy
        OV[2, x] = PR[2, x + 1] - 0.5 * (z_next(mid) - z_prev(mid))
        return 0

    lax.fori_loop(0, 16, correct, 0)

    outs = [
        pltpu.make_async_copy(OV, ov_out, out_sem.at[0]),
        pltpu.make_async_copy(P2.at[pl.ds(1, 16)], p2_out, out_sem.at[1]),
    ]
    for copy in outs:
        copy.start()

    @pl.when((slab >= 6) & (slab <= 9))
    def _():
        @pl.when(side == h)
        def _():
            pltpu.make_async_copy(FB, FA.at[slot, slab], f1r.at[0]).start()

        remote(FA, FA, f1s.at[0], f1r.at[0], slab, cross).wait_recv()

        r_of = (lax.broadcasted_iota(jnp.int32, (5, 16, 128), 0) * 16
                + lax.broadcasted_iota(jnp.int32, (5, 16, 128), 1)).astype(F32).astype(BF16)
        ACC[...] = jnp.zeros(ACC.shape, F32)

        def add(c, _):
            for s in range(16):
                q = (h * 4 + c) * 16 + s
                lanes = pl.ds(s * 128, 128)
                rk = jnp.broadcast_to(RK[pl.ds(q, 1), :], (16, 128)).astype(BF16)[None]
                f = FA[c, s]
                hi = f.astype(BF16).astype(F32)
                lo = f - hi
                mask = r_of == rk
                for i in range(3):
                    for n, part in enumerate((hi, lo)):
                        value = jnp.broadcast_to(part[i:i + 1], (16, 128)).astype(BF16)[None]
                        LHS[pl.ds((i * 2 + n) * 5, 5), :, lanes] = jnp.where(mask, value, jnp.zeros((5, 16, 128), BF16))
            ACC[...] += lax.dot_general(
                LHS[...].reshape(480, 2048), RHS[c].reshape(256, 2048), (((1,), (1,)), ((), ())),
                preferred_element_type=F32,
            )
            return 0

        lax.fori_loop(0, 4, add, 0)

        for i in range(3):
            for p in range(2):
                at = i * 160 + p * 40
                PUSH[i, p] = 0.5 * (ACC[at:at + 40, :] + ACC[at + 80:at + 120, :])
        share = remote(PUSH, PUSH2, f2s.at[0], f2r.at[0], sib, cross)

        @pl.when((slab == 6) | (slab == 9))
        def _():
            share.start()
            share.wait_send()

        @pl.when((slab == 7) | (slab == 8))
        def _():
            share.wait_recv()
            PUSH[...] += PUSH2[...]
            push = pltpu.make_async_copy(PUSH, push_out, out_sem.at[2])
            push.start()
            push.wait()

    for copy in p2_x + p2_y:
        copy.wait_send()
    f1_sends(lambda copy: copy.wait_send())
    for copy in outs:
        copy.wait()


def finish_kernel(ov, p2, push_in, vel_out, pres_out, WV, WP, PUSH, load_sem, out_sem):
    slab = lax.axis_index("slab")
    cross = lax.axis_index("cross")

    def moves(k, into):
        part = pl.ds(4 * k, 4)
        if into:
            return [
                pltpu.make_async_copy(ov.at[:, part], WV.at[:, part], load_sem.at[k]),
                pltpu.make_async_copy(p2.at[part], WP.at[part], load_sem.at[4 + k]),
            ]
        return [
            pltpu.make_async_copy(WV.at[:, part], vel_out.at[:, part], out_sem.at[k]),
            pltpu.make_async_copy(WP.at[part], pres_out.at[part], out_sem.at[4 + k]),
        ]

    def run(first, last):
        if first is not None:
            load = pltpu.make_async_copy(push_in, PUSH, load_sem.at[8])
            load.start()
        order = [k for k in range(4) if k != last] + [last]
        for k in [last] + order[:3]:
            for copy in moves(k, True):
                copy.start()
        for k in order:
            for copy in moves(k, True):
                copy.wait()
            if k == last and first is not None:
                load.wait()
                correct(first, 4 * k, cross, PUSH, WV, WP)
            for copy in moves(k, False):
                copy.start()
        for k in range(4):
            for copy in moves(k, False):
                copy.wait()

    @pl.when(slab == 7)
    def _():
        run(124, 3)

    @pl.when(slab == 8)
    def _():
        run(128, 0)

    @pl.when((slab != 7) & (slab != 8))
    def _():
        run(None, 3)


def correct(first, at, cross, PUSH, WV, WP):
    push = {(i, 127 + p): PUSH[i, p] for i in range(3) for p in range(2)}
    row = lax.broadcasted_iota(jnp.int32, (40, 256), 0) + (cross * 32 - 4)
    inside = (row >= 0) & (row < 256)

    def within(a):
        return jnp.where(inside, a, 0.0)

    def ny(a):
        return pltpu.roll(a, 39, 0)

    def py(a):
        return pltpu.roll(a, 1, 0)

    div = {126: 0.5 * push[0, 127], 129: -0.5 * push[0, 128]}
    for x, side in ((127, push[0, 128]), (128, -push[0, 127])):
        a, b = push[1, x], push[2, x]
        div[x] = within(0.5 * (side + (ny(a) - py(a)) + (z_next(b) - z_prev(b))))
    one = {x: -SIXTH * div[x] for x in div}
    two = {}
    for x in range(125, 131):
        s = None
        if x in one:
            a = one[x]
            s = ny(a) + py(a) + z_next(a) + z_prev(a) - div[x]
        for near in (x - 1, x + 1):
            if near in one:
                s = one[near] if s is None else s + one[near]
        two[x] = within(s * SIXTH)

    def centre(a):
        return pltpu.roll(a, 36, 0)[0:32]

    def apply(first):
        for n in range(4):
            x = first + n
            g = None
            if x + 1 in two:
                g = two[x + 1]
            if x - 1 in two:
                g = -two[x - 1] if g is None else g - two[x - 1]
            vx = -0.5 * g
            if x in (127, 128):
                vx = vx + push[0, x]
            WV[0, at + n] += centre(vx)
            if x in two:
                a = two[x]
                WP[at + n] += centre(a)
                vy = -0.5 * (ny(a) - py(a))
                vz = -0.5 * (z_next(a) - z_prev(a))
                if x in (127, 128):
                    vy = vy + push[1, x]
                    vz = vz + push[2, x]
                WV[1, at + n] += centre(vy)
                WV[2, at + n] += centre(vz)

    apply(first)


def body(velocity, pressure, inv_influence, normals, sample_cells, tangents, force_owner, force_cell):
    any_space = pl.BlockSpec(memory_space=pl.ANY)
    dma = pltpu.SemaphoreType.DMA
    vm = pltpu.VMEM
    ov, p2, push = pl.pallas_call(
        kernel,
        out_shape=(
            jax.ShapeDtypeStruct(velocity.shape, F32),
            jax.ShapeDtypeStruct(pressure.shape, F32),
            jax.ShapeDtypeStruct((3, 2, 40, 256), F32),
        ),
        in_specs=[any_space] * 8,
        out_specs=(any_space,) * 3,
        scratch_shapes=[
            vm((3, 18, 32, 256), F32), vm((18, 32, 256), F32), vm((3, 18, 32, 256), F32),
            vm((18, 32, 256), F32), vm((18, 32, 256), F32), vm((16, 32, 256), F32), vm((3, 16, 32, 256), F32),
            vm((7, 2, 16, 256), F32), vm((7, 2, 16, 256), F32),
            vm((3, 256, 256), F32), vm((384, 512), BF16), vm((2, 8, 128, 1024), BF16), vm((128, 256), jnp.int32),
            vm((2, 64, 256), F32), vm((2, 64, 256), F32), vm((2, 64, 256), jnp.int32),
            pltpu.SMEM((3, 128), F32), vm((3, 1, 1, 128), F32),
            vm((128, 128), jnp.int32), vm((128, 128), jnp.int32), vm((128, 128), F32), vm((128, 128), F32),
            vm((2, 2, 64, 128), F32), vm((2, 8, 2, 64, 128), F32), vm((2, 8, 128, 128), BF16),
            vm((2, 2, 8, 128, 128), F32), vm((2, 8, 128, 128), F32), vm((2, 8, 128, 128), F32),
            vm((3, 128), F32), vm((4, 16, 3, 128), F32),
            vm((30, 16, 2048), BF16), vm((4, 16, 16, 2048), BF16), vm((480, 256), F32), vm((3, 2, 40, 256), F32), vm((3, 2, 40, 256), F32),
            dma((9,)), dma((1,)), dma((3, 16)), dma((3,)), dma((3, 8)), dma((3, 8)), dma((3, 8)), dma((3, 8)),
            dma((2, 8)), dma((2, 8)), dma((2, 8)), dma((2, 8)), dma((2, 8)), dma((2, 8)),
            dma((16,)), dma((1,)), dma((1,)), dma((1,)), dma((5, 2)), dma((5, 2)), dma((7, 2)), dma((7, 2)),
            dma((3,)),
        ],
        compiler_params=pltpu.CompilerParams(
            collective_id=0, has_side_effects=True, vmem_limit_bytes=56 * 1024 * 1024
        ),
    )(
        velocity, pressure, inv_influence.reshape(8, 2, 128, 1024),
        normals.reshape(3, 8, 128).transpose(1, 0, 2), sample_cells, tangents,
        force_owner.reshape(128, 128), force_cell.reshape(128, 128),
    )
    return pl.pallas_call(
        finish_kernel,
        out_shape=(
            jax.ShapeDtypeStruct(velocity.shape, F32),
            jax.ShapeDtypeStruct(pressure.shape, F32),
        ),
        in_specs=[any_space] * 3,
        out_specs=(any_space,) * 2,
        scratch_shapes=[
            vm((3, 16, 32, 256), F32), vm((16, 32, 256), F32), vm((3, 2, 40, 256), F32), dma((9,)), dma((8,)),
        ],
        compiler_params=pltpu.CompilerParams(vmem_limit_bytes=56 * 1024 * 1024),
    )(ov, p2, push)


def solution(mesh):
    return jax.shard_map(
        body,
        mesh=mesh,
        in_specs=(
            P(None, "slab", "cross", None),
            P("slab", "cross", None),
            P("cross", "slab"),
            P(None, "slab"),
            P("slab", None),
            P(None, "cross", "slab", None),
            P(),
            P(),
        ),
        out_specs=(P(None, "slab", "cross", None), P("slab", "cross", None)),
        check_vma=False,
    )
```
